256 devices in a mesh: front: 16 (over z, x_hi), row: 4 (over y), col: 4 (over x_lo, core).
Axes of the slice: x: 4 (x_hi: 2, x_lo: 2; x = x_hi * 2 + x_lo), y: 4, z: 8, core: 2. Of those that a mesh axis runs over, the one named last changes fastest.
Arguments:
- front_matrix: bfloat16 [16, 6144, 6144], P('front', 'row', 'col'), may hold values from -32 to 32, as said below
- kept_child: bfloat16 [16, 2048, 2048], P('front', 'row', 'col'), may hold values from -32 to 32, as said below
- passed_child: bfloat16 [16, 2048, 2048], P('front', 'row', 'col'), may hold values from -32 to 32, as said below
- child_map: int32 [16, 2, 16], P('front'), may hold values from 0 to 47, as said below
- pivots: int32 [16, 2, 4], P('front'), may hold values from 0 to 47, as said below
- pivot_inverse: bfloat16 [16, 2, 512, 512], P('front'), may hold values from -0.03125 to 0.03125, as said below
Outputs:
- updated: bfloat16 [16, 6144, 6144], P('front', 'row', 'col')
The draws below stay inside these ranges and needn't reach their ends.
Inputs may be any that keep to these rules, and one draw needn't show every extreme that they name: `front_matrix`: symmetric in its last two dimensions. `kept_child`: symmetric in its last two dimensions. `passed_child`: symmetric in its last two dimensions. `pivot_inverse`: symmetric in its last two dimensions. `child_map`: within each front and map the entries differ; child block a maps to a parent block p with p // (48 // 4) == a // (16 // 4). `pivots`: entry j of each step lies in block-column range [j * 48 // 4, (j + 1) * 48 // 4); no block is a pivot block twice within a front.
All inputs are finite; a program needn't handle non-finite values.
Results may differ from the reference program's by a relative error of at most 0.0067.
Values may be sent and summed in bfloat16 or wider, within the bound.
No kernel may reach another device: no remote copies, remote signals or barrier semaphores. Data moves between devices by JAX's collectives and lax.ppermute only.
A program may use at most 128 MiB of HBM per device.

```python
import math
import jax
import jax.numpy as jnp
from jax import lax

F = 6144
C = 2048
BLK = 128
P_SIZE = 512
STEPS = 2
FRONTS = 16
NB = 48
CBLK = 16
PB = 4
N_ROW = 4
N_COL = 4


def symmetric(key, leading, extent, spread, lowest, highest):
    sample = jax.random.normal(jax.random.fold_in(key, 11), leading + (extent, extent), jnp.float32)
    paired = (sample + jnp.swapaxes(sample, -1, -2)) * (spread / math.sqrt(2.0))
    factor = jnp.exp(jax.random.uniform(jax.random.fold_in(key, 12), leading + (extent,), jnp.float32, math.log(lowest), math.log(highest)))
    paired = paired * factor[..., :, None] * factor[..., None, :]
    limit = 8.0 * spread
    return jnp.clip(paired, -limit, limit)


def draw_front_matrix(key, part):
    key = jax.random.fold_in(key, 1)
    return symmetric(key, (FRONTS,), F, 1.0, 1.0, 1.0).astype(jnp.bfloat16)


def draw_kept_child(key, part):
    key = jax.random.fold_in(key, 2)
    return symmetric(key, (FRONTS,), C, 1.0, 1.0, 1.0).astype(jnp.bfloat16)


def draw_passed_child(key, part):
    key = jax.random.fold_in(key, 3)
    return symmetric(key, (FRONTS,), C, 1.0, 1.0, 1.0).astype(jnp.bfloat16)


def draw_pivot_inverse(key, part):
    key = jax.random.fold_in(key, 4)
    return symmetric(key, (FRONTS, STEPS), P_SIZE, 0.5 / P_SIZE, 1.0, 1.0).astype(jnp.bfloat16)


def draw_child_map(key, part):
    key = jax.random.fold_in(key, 5)
    blocks_here = NB // N_ROW
    child_blocks = CBLK // N_ROW
    subkeys = jax.random.split(key, FRONTS * 2 * N_ROW)
    shuffled = jax.vmap(lambda single: jax.random.permutation(single, blocks_here))(subkeys)
    picked = jnp.sort(shuffled[:, :child_blocks], axis=1).reshape(FRONTS, 2, N_ROW, child_blocks)
    offsets = (jnp.arange(N_ROW, dtype=jnp.int32) * blocks_here)[None, None, :, None]
    return (picked + offsets).reshape(FRONTS, 2, CBLK).astype(jnp.int32)


def draw_pivots(key, part):
    key = jax.random.fold_in(key, 6)
    blocks_here = NB // N_COL
    subkeys = jax.random.split(key, FRONTS * PB)
    shuffled = jax.vmap(lambda single: jax.random.permutation(single, blocks_here))(subkeys)
    picked = shuffled[:, :STEPS].reshape(FRONTS, PB, STEPS)
    offsets = (jnp.arange(PB, dtype=jnp.int32) * blocks_here)[None, :, None]
    return jnp.swapaxes(picked + offsets, 1, 2).astype(jnp.int32)


def setup_inputs(seed: int = 0) -> dict:
    key_list = jax.random.split(jax.random.key(seed), 7)
    return {
        "front_matrix": draw_front_matrix(jax.random.fold_in(key_list[6], 71), 0),
        "kept_child": draw_kept_child(jax.random.fold_in(key_list[6], 71), 0),
        "passed_child": draw_passed_child(jax.random.fold_in(key_list[6], 71), 0),
        "child_map": draw_child_map(jax.random.fold_in(key_list[6], 71), 0),
        "pivots": draw_pivots(jax.random.fold_in(key_list[6], 71), 0),
        "pivot_inverse": draw_pivot_inverse(jax.random.fold_in(key_list[6], 71), 0),
    }


def extend_add(child, mapping):
    pieces = child.astype(jnp.float32).reshape(CBLK, BLK, CBLK, BLK).transpose(0, 2, 1, 3)
    target = jnp.zeros((NB, NB, BLK, BLK), jnp.float32)
    target = target.at[mapping[:, None], mapping[None, :]].add(pieces)
    return target.transpose(0, 2, 1, 3).reshape(F, F)


def one_front(front, kept, arrived, parent_maps, chosen, inverses):
    current = front.astype(jnp.float32) + extend_add(kept, parent_maps[0]) + extend_add(arrived, parent_maps[1])
    within = jnp.arange(BLK, dtype=jnp.int32)
    for section in range(STEPS):
        columns = (chosen[section][:, None] * BLK + within[None, :]).reshape(P_SIZE).astype(jnp.int32)
        panel_cols = current[:, columns].astype(jnp.bfloat16).astype(jnp.float32)
        inverse_now = inverses[section].astype(jnp.float32)
        multipliers = jnp.dot(panel_cols, inverse_now, precision=lax.Precision.HIGHEST).astype(jnp.bfloat16).astype(jnp.float32)
        current = current - jnp.dot(multipliers, panel_cols.T, precision=lax.Precision.HIGHEST)
    return current.astype(jnp.bfloat16)


def reference(front_matrix, kept_child, passed_child, child_map, pivots, pivot_inverse):
    arrived = passed_child.reshape(FRONTS // 2, 2, C, C)[:, ::-1].reshape(FRONTS, C, C)
    results = []
    for index in range(FRONTS):
        results.append(one_front(front_matrix[index], kept_child[index], arrived[index], child_map[index], pivots[index], pivot_inverse[index]))
    return jnp.stack(results)
```

```python
import jax
import jax.numpy as jnp
from jax import lax
from jax.experimental import pallas as pl
from jax.experimental.pallas import tpu as pltpu
from jax.sharding import PartitionSpec as P

BLK = 128
PAIR = 2 * BLK
P_SIZE = 512
F32 = jnp.float32
BF16 = jnp.bfloat16
VMEM = pl.BlockSpec(memory_space=pltpu.VMEM)
HBM = pl.BlockSpec(memory_space=pltpu.HBM)
MIB = 1 << 20
SMALL = pl.CostEstimate(flops=1000, bytes_accessed=1000, transcendentals=0)


def shift(x, axis, step):
    n = lax.axis_size(axis)
    return lax.ppermute(x, axis, [(i, (i + step) % n) for i in range(n)])


def flip(x, axis, bit):
    n = lax.axis_size(axis)
    return lax.ppermute(x, axis, [(i, i ^ bit) for i in range(n)])


def at(block, size=BLK):
    return pl.ds(pl.multiple_of(block * size, size), size)


def places():
    return lax.axis_index("row"), lax.axis_index("col")


def dot(a, b):
    return jnp.dot(a, b, preferred_element_type=F32)


def dot_t(a, b):
    return lax.dot_general(a, b, (((1,), (1,)), ((), ())), preferred_element_type=F32)


def out(*shape, dtype=BF16):
    return jax.ShapeDtypeStruct(shape, dtype)


def params(mib):
    return pltpu.CompilerParams(vmem_limit_bytes=mib * MIB)


def add_rows(acc, child, which, s, map_s, piv_s, row, col, here, kids):
    for k in range(kids):

        @pl.when(map_s[0, which, row * kids + k] == piv_s[0, s, row])
        def _():
            for a in range(kids):
                t = map_s[0, which, col * kids + a] - col * here
                acc[s, :, at(t)] += child[0, k * BLK : (k + 1) * BLK, a * BLK : (a + 1) * BLK].astype(F32)


def add_cols(acc, child, which, s, map_s, piv_s, row, col, here, kids):
    for k in range(kids):

        @pl.when(map_s[0, which, col * kids + k] == piv_s[0, s, col])
        def _():
            for a in range(kids):
                t = map_s[0, which, row * kids + a] - row * here
                acc[s, at(t), :] += child[0, a * BLK : (a + 1) * BLK, k * BLK : (k + 1) * BLK].astype(F32)


def scalars(map_ref, piv_ref, map_s, piv_s, sem):
    first = pltpu.make_async_copy(map_ref, map_s, sem.at[0])
    second = pltpu.make_async_copy(piv_ref, piv_s, sem.at[1])
    first.start()
    second.start()
    first.wait()
    second.wait()


def each_block(map_s, col, here, kids, visit):
    place = jnp.int32(0)
    for t in range(here):
        hit = jnp.bool_(False)
        for a in range(kids):
            hit = hit | (map_s[0, 1, col * kids + a] - col * here == t)

        @pl.when(jnp.logical_not(hit))
        def _():
            visit(t, place)

        place = place + jnp.where(hit, 0, 1)


def early_kernel(map_ref, piv_ref, front, kept, rows_out, map_s, piv_s, rows_in, kid, sem):
    row, col = places()
    here = front.shape[1] // BLK
    kids = kept.shape[1] // BLK
    child = pltpu.make_async_copy(kept, kid, sem.at[2])
    child.start()
    scalars(map_ref, piv_ref, map_s, piv_s, sem)
    copies = []
    for s in range(2):
        pr = piv_s[0, s, row] - row * here
        copies.append(pltpu.make_async_copy(front.at[0, at(pr), :], rows_in.at[s], sem.at[s]))
    for c in copies:
        c.start()
    for c in copies:
        c.wait()
    child.wait()
    for s in range(2):
        for k in range(kids):

            @pl.when(map_s[0, 0, row * kids + k] == piv_s[0, s, row])
            def _():
                for a in range(kids):
                    t = at(map_s[0, 0, col * kids + a] - col * here)
                    piece = kid[0, k * BLK : (k + 1) * BLK, a * BLK : (a + 1) * BLK].astype(F32)
                    rows_in[s, :, t] = (rows_in[s, :, t].astype(F32) + piece).astype(BF16)

    def visit(t, place):
        for s in range(2):
            rows_out[s * BLK : (s + 1) * BLK, at(place)] = rows_in[s, :, t * BLK : (t + 1) * BLK]

    each_block(map_s, col, here, kids, visit)


def early(child_map, pivots, front, kept):
    span = front.shape[1]
    return pl.pallas_call(
        early_kernel,
        out_shape=out(PAIR, span - kept.shape[1]),
        in_specs=[HBM] * 4,
        out_specs=VMEM,
        scratch_shapes=[
            pltpu.SMEM(child_map.shape, jnp.int32),
            pltpu.SMEM(pivots.shape, jnp.int32),
            pltpu.VMEM((2, BLK, span), BF16),
            pltpu.VMEM(kept.shape, BF16),
            pltpu.SemaphoreType.DMA((3,)),
        ],
        compiler_params=params(57),
        cost_estimate=SMALL,
        name="early",
    )(child_map, pivots, front, kept)


def prepare_kernel(
    map_ref, piv_ref, front, kept, rows_out, cols32, map_s, piv_s, rows_in, cols_in, rows32, sem
):
    row, col = places()
    here = front.shape[1] // BLK
    kids = kept.shape[1] // BLK
    scalars(map_ref, piv_ref, map_s, piv_s, sem)
    copies = []
    for s in range(2):
        pr = piv_s[0, s, row] - row * here
        pc = piv_s[0, s, col] - col * here
        copies.append(pltpu.make_async_copy(front.at[0, at(pr), :], rows_in.at[s], sem.at[2 * s]))
        copies.append(pltpu.make_async_copy(front.at[0, :, at(pc)], cols_in.at[s], sem.at[2 * s + 1]))
    for c in copies:
        c.start()
    for c in copies:
        c.wait()
    rows32[...] = rows_in[...].astype(F32)
    cols32[...] = cols_in[...].astype(F32)
    for s in range(2):
        add_rows(rows32, kept, 0, s, map_s, piv_s, row, col, here, kids)
        add_cols(cols32, kept, 0, s, map_s, piv_s, row, col, here, kids)
        for a in range(kids):
            t = map_s[0, 1, col * kids + a] - col * here
            rows_out[s, :, a * BLK : (a + 1) * BLK] = rows32[s, :, at(t)]


def prepare(child_map, pivots, front, kept):
    span = front.shape[1]
    return pl.pallas_call(
        prepare_kernel,
        out_shape=(out(2, BLK, kept.shape[1], dtype=F32), out(2, span, BLK, dtype=F32)),
        in_specs=[HBM, HBM, HBM, VMEM],
        out_specs=(VMEM, VMEM),
        scratch_shapes=[
            pltpu.SMEM(child_map.shape, jnp.int32),
            pltpu.SMEM(pivots.shape, jnp.int32),
            pltpu.VMEM((2, BLK, span), BF16),
            pltpu.VMEM((2, span, BLK), BF16),
            pltpu.VMEM((2, BLK, span), F32),
            pltpu.SemaphoreType.DMA((4,)),
        ],
        compiler_params=params(12),
        cost_estimate=SMALL,
        name="prepare",
    )(child_map, pivots, front, kept)


def extract_kernel(map_s, piv_s, rows32, cols32, arrived, rows_out, top, bottom, cross):
    row, col = places()
    half = top.shape[0]
    halves = half // BLK
    here = 2 * halves
    kids = arrived.shape[1] // BLK
    for s in range(2):
        own = slice(s * BLK, (s + 1) * BLK)
        rows_out[own, : kids * BLK] = rows32[s].astype(BF16)
        top[:, own] = cols32[s, :half].astype(BF16)
        bottom[:, own] = cols32[s, half:].astype(BF16)
        for k in range(kids):

            @pl.when(map_s[0, 1, row * kids + k] == piv_s[0, s, row])
            def _():
                piece = arrived[0, k * BLK : (k + 1) * BLK, :].astype(F32)
                rows_out[own, : kids * BLK] = (rows32[s] + piece).astype(BF16)

            @pl.when(map_s[0, 1, col * kids + k] == piv_s[0, s, col])
            def _():
                for a in range(kids):
                    t = map_s[0, 1, row * kids + a] - row * here
                    piece = arrived[0, a * BLK : (a + 1) * BLK, k * BLK : (k + 1) * BLK].astype(F32)
                    total = (cols32[s, at(t), :] + piece).astype(BF16)

                    @pl.when(t < halves)
                    def _():
                        top[at(t), own] = total

                    @pl.when(t >= halves)
                    def _():
                        bottom[at(t - halves), own] = total

    t = piv_s[0, 1, row] - row * here
    rows_out[BLK:, kids * BLK :] = jnp.zeros((BLK, BLK), BF16)

    @pl.when(t < halves)
    def _():
        rows_out[:BLK, kids * BLK :] = top[at(t), :BLK]
        cross[...] = top[at(t), :BLK]

    @pl.when(t >= halves)
    def _():
        rows_out[:BLK, kids * BLK :] = bottom[at(t - halves), :BLK]
        cross[...] = bottom[at(t - halves), :BLK]


def extract(child_map, pivots, rows32, cols32, arrived):
    half = cols32.shape[1] // 2
    return pl.pallas_call(
        extract_kernel,
        out_shape=(out(PAIR, arrived.shape[1] + BLK), out(half, PAIR), out(half, PAIR), out(BLK, BLK)),
        in_specs=[pl.BlockSpec(memory_space=pltpu.SMEM)] * 2 + [VMEM] * 3,
        out_specs=(VMEM,) * 4,
        compiler_params=params(8),
        cost_estimate=SMALL,
        name="extract",
    )(child_map, pivots, rows32, cols32, arrived)


def base_kernel(map_ref, front, kept, arrived, base, map_s, sem):
    row, col = places()
    step = pl.program_id(0)
    here = front.shape[2] // BLK
    deep = front.shape[1] // BLK
    kids = kept.shape[1] // BLK
    width = front.shape[1]
    load = pltpu.make_async_copy(map_ref, map_s, sem.at[0])
    load.start()
    load.wait()
    mine = pl.ds(pl.multiple_of(step * width, width), width)
    base[mine, :] = front[0].astype(F32)
    for which, child in ((0, kept), (1, arrived)):
        for k in range(kids):
            t = map_s[0, which, row * kids + k] - row * here - step * deep

            @pl.when((t >= 0) & (t < deep))
            def _():
                for a in range(kids):
                    u = map_s[0, which, col * kids + a] - col * here
                    piece = child[0, k * BLK : (k + 1) * BLK, a * BLK : (a + 1) * BLK]
                    base[at(t + step * deep), at(u)] += piece.astype(F32)


def make_base(child_map, front, kept, arrived):
    span = front.shape[1]
    steps = 4
    return pl.pallas_call(
        base_kernel,
        grid=(steps,),
        out_shape=out(span, span, dtype=F32),
        in_specs=[HBM, pl.BlockSpec((1, span // steps, span), lambda i: (0, i, 0)), VMEM, VMEM],
        out_specs=VMEM,
        scratch_shapes=[pltpu.SMEM(child_map.shape, jnp.int32), pltpu.SemaphoreType.DMA((1,))],
        compiler_params=params(16),
        cost_estimate=SMALL,
        name="base",
    )(child_map, front, kept, arrived)


def weights_kernel(x0, x1, x2, x3, inverse, w, x, k, ki):
    row, col = places()
    for q, xq in enumerate((x0, x1, x2, x3)):
        j = lax.bitwise_xor(col, q)
        for d in range(4):
            x[at(lax.rem(row + d, 4)), at(j)] = xq[d]
    k[...] = dot_t(inverse[0, 0], x[...]).astype(BF16)
    ki[...] = dot(k[...], inverse[0, 1]).astype(BF16)
    both = (inverse[0, 0].astype(F32) + dot_t(ki[...], k[...])).astype(BF16)
    flat = dot_t(inverse[0, 1], k[...]).astype(BF16)
    for i in range(4):
        for j in range(4):
            a, b = slice(i * BLK, (i + 1) * BLK), slice(j * BLK, (j + 1) * BLK)
            upper, lower = slice(i * PAIR, i * PAIR + BLK), slice(i * PAIR + BLK, (i + 1) * PAIR)
            left, right = slice(j * PAIR, j * PAIR + BLK), slice(j * PAIR + BLK, (j + 1) * PAIR)
            w[upper, left] = both[a, b]
            w[upper, right] = -ki[a, b]
            w[lower, left] = -flat[a, b]
            w[lower, right] = inverse[0, 1, a, b]


def weights(crosses, inverse):
    return pl.pallas_call(
        weights_kernel,
        out_shape=out(2 * P_SIZE, 2 * P_SIZE),
        in_specs=[VMEM] * 5,
        out_specs=VMEM,
        scratch_shapes=[pltpu.VMEM((P_SIZE, P_SIZE), BF16)] * 3,
        compiler_params=params(12),
        cost_estimate=SMALL,
        name="weights",
    )(*crosses, inverse)


def gather_kernel(w, u0, u1, u3, a0, a1, a3, acc):
    row, _ = places()
    split = u0.shape[1]
    js = [lax.rem(row + d, 4) for d in (0, 1, 3)]

    def chunk(pieces, n, offset):
        here = at(n, PAIR)
        total = dot(w[:, at(js[0], PAIR)], pieces[0][:, here])
        total += dot(w[:, at(js[1], PAIR)], pieces[1][:, here])
        total += dot(w[:, at(js[2], PAIR)], pieces[2][:, here])
        acc[:, at(n + offset, PAIR)] = total

    @pl.loop(0, split // PAIR)
    def _(n):
        chunk((u0, u1, u3), n, 0)

    @pl.loop(0, acc.shape[1] // PAIR - split // PAIR)
    def _(n):
        chunk((a0, a1, a3), n, split // PAIR)


def gather(w, us, as_, span):
    return pl.pallas_call(
        gather_kernel,
        out_shape=out(2 * P_SIZE, span, dtype=F32),
        in_specs=[VMEM] * 7,
        out_specs=VMEM,
        compiler_params=params(12),
        cost_estimate=SMALL,
        name="gather",
    )(w, *us, *as_)


def finish_kernel(map_ref, w, acc, f1, f2, v, map_s, order, far, sem):
    row, col = places()
    span = acc.shape[1]
    here = span // BLK
    kids = map_s.shape[2] // 4
    load = pltpu.make_async_copy(map_ref, map_s, sem.at[0])
    load.start()
    far[:BLK, :] = f1[...]
    far[BLK:, :] = f2[...]
    load.wait()

    def visit(t, place):
        order[place] = t

    each_block(map_s, col, here, kids, visit)
    for a in range(kids):
        order[here - kids + a] = map_s[0, 1, col * kids + a] - col * here
    mine = at(lax.rem(row + 2, 4), PAIR)

    @pl.loop(0, span // PAIR)
    def _(n):
        chunk = at(n, PAIR)
        total = (acc[:, chunk] + dot(w[:, mine], far[:, chunk])).astype(BF16)
        v[:, at(order[2 * n])] = total[:, :BLK]
        v[:, at(order[2 * n + 1])] = total[:, BLK:]


def finish(child_map, w, acc, f1, f2):
    return pl.pallas_call(
        finish_kernel,
        out_shape=out(*acc.shape),
        in_specs=[HBM] + [VMEM] * 4,
        out_specs=VMEM,
        scratch_shapes=[
            pltpu.SMEM(child_map.shape, jnp.int32),
            pltpu.SMEM((acc.shape[1] // BLK,), jnp.int32),
            pltpu.VMEM((PAIR, acc.shape[1]), BF16),
            pltpu.SemaphoreType.DMA((1,)),
        ],
        compiler_params=params(8),
        cost_estimate=SMALL,
        name="finish",
    )(child_map, w, acc, f1, f2)


def update_kernel(half, c0, c1, c2, c3, v, base, updated, panel, done, sem):
    _, col = places()
    depth = c0.shape[0]
    width = done.shape[2]
    rows = pl.ds(half * depth, depth)
    for q, c in enumerate((c0, c1, c2, c3)):
        panel[:, at(lax.bitwise_xor(col, q), PAIR)] = c[...]

    def store(n):
        return pltpu.make_async_copy(done.at[n], updated.at[0, rows, at(n, width)], sem.at[n])

    chunks = done.shape[0]

    @pl.loop(0, chunks)
    def _(n):
        here = at(n, width)
        done[n] = (base[rows, here] - dot(panel[...], v[:, here])).astype(BF16)
        store(n).start()

    @pl.loop(0, chunks)
    def _(n):
        store(n).wait()


def update(half, pieces, v, base, *rest):
    span = base.shape[0]
    width = 2 * PAIR

    def kernel(*refs):
        update_kernel(half, *refs[:6], *refs[6 + len(rest) :])

    return pl.pallas_call(
        kernel,
        out_shape=out(1, span, span),
        in_specs=[VMEM] * 6 + [HBM] * len(rest),
        out_specs=HBM,
        input_output_aliases={6: 0} if rest else {},
        scratch_shapes=[
            pltpu.VMEM((span // 2, 4 * PAIR), BF16),
            pltpu.VMEM((span // width, span // 2, width), BF16),
            pltpu.SemaphoreType.DMA((span // width,)),
        ],
        compiler_params=params(12),
        cost_estimate=SMALL,
        name="update",
    )(*pieces, v, base, *rest)


def body(front_matrix, kept_child, passed_child, child_map, pivots, pivot_inverse):
    hold = lax.optimization_barrier
    span = front_matrix.shape[1]
    kid = kept_child.shape[1]
    arrived = flip(passed_child, "front", 1)
    u = early(child_map, pivots, front_matrix, kept_child)
    un, up = shift(u, "row", -1), shift(u, "row", 1)
    rows32, cols32 = prepare(child_map, pivots, front_matrix, kept_child)
    arrived, _, rows32, cols32 = hold((arrived, u, rows32, cols32))
    a, top, bottom, cross = extract(child_map, pivots, rows32, cols32, arrived)
    tfar, tnear = flip(top, "col", 2), flip(top, "col", 1)
    an, ap = shift(a, "row", -1), shift(a, "row", 1)
    cross2 = shift(cross, "row", 2)
    base = make_base(child_map, front_matrix, kept_child, arrived)
    un, up, an, ap, cross2, base, tfar, tnear = hold((un, up, an, ap, cross2, base, tfar, tnear))
    crosses = jnp.stack([cross, an[:BLK, kid:], cross2, ap[:BLK, kid:]])
    xfar, xnear = flip(crosses, "col", 2), flip(crosses, "col", 1)
    f1 = shift(jnp.concatenate([up[:BLK], ap[:BLK, :kid]], axis=1), "row", 1)
    f2 = shift(jnp.concatenate([un[BLK:], an[BLK:, :kid]], axis=1), "row", -1)
    tcorner = flip(tfar, "col", 1)
    xfar, xnear, tcorner, bottom = hold((xfar, xnear, tcorner, bottom))
    xcorner = flip(xfar, "col", 1)
    bfar, bnear = flip(bottom, "col", 2), flip(bottom, "col", 1)
    w = weights((crosses, xnear, xfar, xcorner), pivot_inverse)
    acc = gather(w, (u, un, up), (a, an, ap), span)
    acc, f1, f2 = hold((acc, f1, f2))
    v = finish(child_map, w, acc, f1, f2)
    v, bfar, bnear = hold((v, bfar, bnear))
    bcorner = flip(bfar, "col", 1)
    upper = update(0, (top, tnear, tfar, tcorner), v, base)
    upper, bcorner = hold((upper, bcorner))
    return update(1, (bottom, bnear, bfar, bcorner), v, base, upper)


def solution(mesh):
    in_specs = (
        P("front", "row", "col"),
        P("front", "row", "col"),
        P("front", "row", "col"),
        P("front", None, None),
        P("front", None, None),
        P("front", None, None, None),
    )
    out_specs = P("front", "row", "col")
    return jax.shard_map(body, mesh=mesh, in_specs=in_specs, out_specs=out_specs, check_vma=False)
```

```python
import jax
import jax.numpy as jnp
from jax import lax
from jax.experimental import pallas as pl
from jax.experimental.pallas import tpu as pltpu
from jax.sharding import PartitionSpec as P

BLK = 128
PAIR = 2 * BLK
TILE = 512
P_SIZE = 512
F32 = jnp.float32
BF16 = jnp.bfloat16
VMEM = pl.BlockSpec(memory_space=pltpu.VMEM)
HBM = pl.BlockSpec(memory_space=pltpu.HBM)
SMEM = pl.BlockSpec(memory_space=pltpu.SMEM)
MIB = 1 << 20
SMALL = pl.CostEstimate(flops=1000, bytes_accessed=1000, transcendentals=0)


def shift(x, axis, step):
    n = lax.axis_size(axis)
    return lax.ppermute(x, axis, [(i, (i + step) % n) for i in range(n)])


def flip(x, axis, bit):
    n = lax.axis_size(axis)
    return lax.ppermute(x, axis, [(i, i ^ bit) for i in range(n)])


def at(block, size=BLK):
    return pl.ds(pl.multiple_of(block * size, size), size)


def places():
    return lax.axis_index("row"), lax.axis_index("col")


def dot(a, b):
    return jnp.dot(a, b, preferred_element_type=F32)


def dot_t(a, b):
    return lax.dot_general(a, b, (((1,), (1,)), ((), ())), preferred_element_type=F32)


def out(*shape, dtype=BF16):
    return jax.ShapeDtypeStruct(shape, dtype)


def params(mib):
    return pltpu.CompilerParams(vmem_limit_bytes=mib * MIB)


def add_rows(acc, child, which, s, map_s, piv_s, row, col, here, kids):
    for k in range(kids):

        @pl.when(map_s[0, which, row * kids + k] == piv_s[0, s, row])
        def _():
            for a in range(kids):
                t = map_s[0, which, col * kids + a] - col * here
                acc[s, :, at(t)] += child[0, k * BLK : (k + 1) * BLK, a * BLK : (a + 1) * BLK].astype(F32)


def add_cols(acc, child, which, s, map_s, piv_s, row, col, here, kids):
    for k in range(kids):

        @pl.when(map_s[0, which, col * kids + k] == piv_s[0, s, col])
        def _():
            for a in range(kids):
                t = map_s[0, which, row * kids + a] - row * here
                acc[s, at(t), :] += child[0, a * BLK : (a + 1) * BLK, k * BLK : (k + 1) * BLK].astype(F32)


def scalars(map_ref, piv_ref, map_s, piv_s, sem):
    first = pltpu.make_async_copy(map_ref, map_s, sem.at[0])
    second = pltpu.make_async_copy(piv_ref, piv_s, sem.at[1])
    first.start()
    second.start()
    first.wait()
    second.wait()


def each_block(map_s, col, here, kids, visit):
    place = jnp.int32(0)
    for t in range(here):
        hit = jnp.bool_(False)
        for a in range(kids):
            hit = hit | (map_s[0, 1, col * kids + a] - col * here == t)

        @pl.when(jnp.logical_not(hit))
        def _():
            visit(t, place)

        place = place + jnp.where(hit, 0, 1)


def early_kernel(map_ref, piv_ref, front, kept, rows_out, map_s, piv_s, rows_in, kid, sem):
    row, col = places()
    here = front.shape[1] // BLK
    kids = kept.shape[1] // BLK
    child = pltpu.make_async_copy(kept, kid, sem.at[2])
    child.start()
    scalars(map_ref, piv_ref, map_s, piv_s, sem)
    copies = []
    for s in range(2):
        pr = piv_s[0, s, row] - row * here
        copies.append(pltpu.make_async_copy(front.at[0, at(pr), :], rows_in.at[s], sem.at[s]))
    for c in copies:
        c.start()
    for c in copies:
        c.wait()
    child.wait()
    for s in range(2):
        for k in range(kids):

            @pl.when(map_s[0, 0, row * kids + k] == piv_s[0, s, row])
            def _():
                for a in range(kids):
                    t = at(map_s[0, 0, col * kids + a] - col * here)
                    piece = kid[0, k * BLK : (k + 1) * BLK, a * BLK : (a + 1) * BLK].astype(F32)
                    rows_in[s, :, t] = (rows_in[s, :, t].astype(F32) + piece).astype(BF16)

    def visit(t, place):
        for s in range(2):
            rows_out[s * BLK : (s + 1) * BLK, at(place)] = rows_in[s, :, t * BLK : (t + 1) * BLK]

    each_block(map_s, col, here, kids, visit)


def early(child_map, pivots, front, kept):
    span = front.shape[1]
    return pl.pallas_call(
        early_kernel,
        out_shape=out(PAIR, span - kept.shape[1]),
        in_specs=[HBM] * 4,
        out_specs=VMEM,
        scratch_shapes=[
            pltpu.SMEM(child_map.shape, jnp.int32),
            pltpu.SMEM(pivots.shape, jnp.int32),
            pltpu.VMEM((2, BLK, span), BF16),
            pltpu.VMEM(kept.shape, BF16),
            pltpu.SemaphoreType.DMA((3,)),
        ],
        compiler_params=params(57),
        cost_estimate=SMALL,
        name="early",
    )(child_map, pivots, front, kept)


def prepare_kernel(
    map_ref, piv_ref, front, kept, rows_out, cols32, map_s, piv_s, rows_in, cols_in, rows32, sem
):
    row, col = places()
    here = front.shape[1] // BLK
    kids = kept.shape[1] // BLK
    scalars(map_ref, piv_ref, map_s, piv_s, sem)
    copies = []
    for s in range(2):
        pr = piv_s[0, s, row] - row * here
        pc = piv_s[0, s, col] - col * here
        copies.append(pltpu.make_async_copy(front.at[0, at(pr), :], rows_in.at[s], sem.at[2 * s]))
        copies.append(pltpu.make_async_copy(front.at[0, :, at(pc)], cols_in.at[s], sem.at[2 * s + 1]))
    for c in copies:
        c.start()
    for c in copies:
        c.wait()
    rows32[...] = rows_in[...].astype(F32)
    cols32[...] = cols_in[...].astype(F32)
    for s in range(2):
        add_rows(rows32, kept, 0, s, map_s, piv_s, row, col, here, kids)
        add_cols(cols32, kept, 0, s, map_s, piv_s, row, col, here, kids)
        for a in range(kids):
            t = map_s[0, 1, col * kids + a] - col * here
            rows_out[s, :, a * BLK : (a + 1) * BLK] = rows32[s, :, at(t)]


def prepare(child_map, pivots, front, kept):
    span = front.shape[1]
    return pl.pallas_call(
        prepare_kernel,
        out_shape=(out(2, BLK, kept.shape[1], dtype=F32), out(2, span, BLK, dtype=F32)),
        in_specs=[HBM, HBM, HBM, VMEM],
        out_specs=(VMEM, VMEM),
        scratch_shapes=[
            pltpu.SMEM(child_map.shape, jnp.int32),
            pltpu.SMEM(pivots.shape, jnp.int32),
            pltpu.VMEM((2, BLK, span), BF16),
            pltpu.VMEM((2, span, BLK), BF16),
            pltpu.VMEM((2, BLK, span), F32),
            pltpu.SemaphoreType.DMA((4,)),
        ],
        compiler_params=params(12),
        cost_estimate=SMALL,
        name="prepare",
    )(child_map, pivots, front, kept)


def extract_kernel(map_s, piv_s, rows32, cols32, arrived, rows_out, top, bottom, cross, cols):
    row, col = places()
    here = cols.shape[0] // BLK
    kids = arrived.shape[1] // BLK
    for s in range(2):
        own = slice(s * BLK, (s + 1) * BLK)
        rows_out[own, : kids * BLK] = rows32[s].astype(BF16)
        cols[:, own] = cols32[s].astype(BF16)
        for k in range(kids):

            @pl.when(map_s[0, 1, row * kids + k] == piv_s[0, s, row])
            def _():
                piece = arrived[0, k * BLK : (k + 1) * BLK, :].astype(F32)
                rows_out[own, : kids * BLK] = (rows32[s] + piece).astype(BF16)

            @pl.when(map_s[0, 1, col * kids + k] == piv_s[0, s, col])
            def _():
                for a in range(kids):
                    t = map_s[0, 1, row * kids + a] - row * here
                    piece = arrived[0, a * BLK : (a + 1) * BLK, k * BLK : (k + 1) * BLK].astype(F32)
                    cols[at(t), own] = (cols32[s, at(t), :] + piece).astype(BF16)

    top[...] = cols[: top.shape[0], :]
    bottom[...] = cols[top.shape[0] :, :]
    block = cols[at(piv_s[0, 1, row] - row * here), :BLK]
    rows_out[:BLK, kids * BLK :] = block
    rows_out[BLK:, kids * BLK :] = jnp.zeros((BLK, BLK), BF16)
    cross[...] = block


def extract(child_map, pivots, rows32, cols32, arrived):
    span = cols32.shape[1]
    return pl.pallas_call(
        extract_kernel,
        out_shape=(
            out(PAIR, arrived.shape[1] + BLK),
            out(span - TILE, PAIR),
            out(TILE, PAIR),
            out(BLK, BLK),
        ),
        in_specs=[SMEM] * 2 + [VMEM] * 3,
        out_specs=(VMEM,) * 4,
        scratch_shapes=[pltpu.VMEM((span, PAIR), BF16)],
        compiler_params=params(8),
        cost_estimate=SMALL,
        name="extract",
    )(child_map, pivots, rows32, cols32, arrived)


def add_blocks(base, child, which, map_s, first, deep):
    row, col = places()
    here = base.shape[1] // BLK
    kids = child.shape[1] // BLK
    for k in range(kids):
        t = map_s[0, which, row * kids + k] - row * here

        @pl.when((t >= first) & (t < first + deep))
        def _():
            for a in range(kids):
                u = map_s[0, which, col * kids + a] - col * here
                piece = child[0, k * BLK : (k + 1) * BLK, a * BLK : (a + 1) * BLK]
                base[at(t), at(u)] += piece.astype(F32)


def make_base(child_map, front, kept):
    span = front.shape[1]
    steps = 4
    width = span // steps

    def kernel(map_s, front, kept, base):
        step = pl.program_id(0)
        base[at(step, width), :] = front[0].astype(F32)
        add_blocks(base, kept, 0, map_s, step * (width // BLK), width // BLK)

    return pl.pallas_call(
        kernel,
        grid=(steps,),
        out_shape=out(span, span, dtype=F32),
        in_specs=[SMEM, pl.BlockSpec((1, width, span), lambda i: (0, i, 0)), VMEM],
        out_specs=VMEM,
        compiler_params=params(14),
        cost_estimate=SMALL,
        name="base",
    )(child_map, front, kept)


def add_child(child_map, base, arrived):
    def kernel(map_s, _, arrived, base):
        add_blocks(base, arrived, 1, map_s, 0, base.shape[0] // BLK)

    return pl.pallas_call(
        kernel,
        out_shape=out(*base.shape, dtype=F32),
        in_specs=[SMEM, VMEM, VMEM],
        out_specs=VMEM,
        input_output_aliases={1: 0},
        compiler_params=params(4),
        cost_estimate=SMALL,
        name="add_child",
    )(child_map, base, arrived)


def stage(us, as_):
    split = us[0].shape[1]
    kid = as_[0].shape[1] - BLK

    def kernel(u0, u1, u2, a0, a1, a2, panel, onward):
        _, col = places()
        even = lax.rem(col, 2) == 0
        for n, (u, a) in enumerate(((u0, a0), (u1, a1), (u2, a2))):
            panel[n * PAIR : (n + 1) * PAIR, :split] = u[...]
            panel[n * PAIR : (n + 1) * PAIR, split:] = a[:, :kid]

        @pl.when(even)
        def _():
            onward[:, :split] = u2[...]
            onward[:, split:] = a2[:, :kid]

        @pl.when(jnp.logical_not(even))
        def _():
            onward[:, :split] = u1[...]
            onward[:, split:] = a1[:, :kid]

    return pl.pallas_call(
        kernel,
        out_shape=(out(2 * P_SIZE, split + kid), out(PAIR, split + kid)),
        in_specs=[VMEM] * 6,
        out_specs=(VMEM, VMEM),
        compiler_params=params(4),
        cost_estimate=SMALL,
        name="stage",
    )(*us, *as_)


def hand_on(x):
    rows, cols = lax.axis_size("row"), lax.axis_size("col")
    route = []
    for r in range(rows):
        for c in range(cols):
            to = (r + 1) % rows if c % 2 == 0 else (r - 1) % rows
            route.append((r * cols + c, to * cols + c))
    return lax.ppermute(x, ("row", "col"), route)


def begin(pieces, corners, inverse):
    span = pieces[0].shape[0]

    def kernel(c0, c1, c2, k0, k1, inverse, first, second):
        _, col = places()
        js = [lax.bitwise_xor(col, q) for q in range(4)]
        for n, corner in enumerate((k0, k1)):
            rows = slice(n * TILE, (n + 1) * TILE)
            total = dot(corner[:, :BLK], inverse[0, 0, at(js[3]), :])
            second[rows, at(js[3])] = corner[:, BLK:]
            for q, c in enumerate((c0, c1, c2)):
                total += dot(c[rows, :BLK], inverse[0, 0, at(js[q]), :])
                second[rows, at(js[q])] = c[rows, BLK:]
            first[rows, :] = total

    return pl.pallas_call(
        kernel,
        out_shape=(out(span, P_SIZE, dtype=F32), out(span, P_SIZE)),
        in_specs=[VMEM] * 6,
        out_specs=(VMEM, VMEM),
        compiler_params=params(6),
        cost_estimate=SMALL,
        name="begin",
    )(*pieces, *corners, inverse)


def ring_places(row):
    found = []
    for j in range(4):
        d = lax.rem(j - row + 4, 4)
        found.append(jnp.where(d < 2, d, 5 - d))
    return found


def eliminate(mult, rows, m1, i2, x, k, inverse, place):
    p2 = (i2.astype(F32) - dot_t(m1.astype(BF16), x[...])).astype(BF16)
    m2 = dot(p2, inverse[0, 1]).astype(BF16)
    n1 = (m1 - dot_t(m2, k[...])).astype(BF16)
    for j in range(4):
        b = slice(j * BLK, (j + 1) * BLK)
        mult[rows, at(2 * place[j])] = n1[:, b]
        mult[rows, at(2 * place[j] + 1)] = m2[:, b]


def multiply_top(crosses, first, second, inverse):
    span = first.shape[0]

    def kernel(x0, x1, x2, x3, x4, first, second, inverse, mult, x, k):
        row, col = places()
        for q, xq in enumerate((x0, x1, x2, (x3, x4))):
            j = lax.bitwise_xor(col, q)
            for d in range(4):
                x[at(lax.rem(row + d, 4)), at(j)] = xq[d // 2][d % 2] if q == 3 else xq[d]
        k[...] = dot_t(inverse[0, 0], x[...]).astype(BF16)
        place = ring_places(row)
        for r in range(0, span, TILE):
            rows = slice(r, r + TILE)
            eliminate(mult, rows, first[rows, :], second[rows, :], x, k, inverse, place)

    return pl.pallas_call(
        kernel,
        out_shape=(out(span, 2 * P_SIZE), out(P_SIZE, P_SIZE), out(P_SIZE, P_SIZE)),
        in_specs=[VMEM] * 8,
        out_specs=(VMEM,) * 3,
        compiler_params=params(8),
        cost_estimate=SMALL,
        name="multiply_top",
    )(*crosses, first, second, inverse)


def multiply_bottom(pieces, corners, x, k, inverse):
    span = pieces[0].shape[0]

    def kernel(c0, c1, c2, k0, k1, x, k, inverse, mult, p1, i2):
        row, col = places()
        for q, c in enumerate((c0, c1, c2)):
            j = lax.bitwise_xor(col, q)
            p1[:, at(j)] = c[:, :BLK]
            i2[:, at(j)] = c[:, BLK:]
        j = lax.bitwise_xor(col, 3)
        for n, corner in enumerate((k0, k1)):
            rows = slice(n * PAIR, (n + 1) * PAIR)
            p1[rows, at(j)] = corner[:, :BLK]
            i2[rows, at(j)] = corner[:, BLK:]
        m1 = dot(p1[...], inverse[0, 0])
        eliminate(mult, slice(0, span), m1, i2[...], x, k, inverse, ring_places(row))

    return pl.pallas_call(
        kernel,
        out_shape=out(span, 2 * P_SIZE),
        in_specs=[VMEM] * 8,
        out_specs=VMEM,
        scratch_shapes=[pltpu.VMEM((span, P_SIZE), BF16)] * 2,
        compiler_params=params(8),
        cost_estimate=SMALL,
        name="multiply_bottom",
    )(*pieces, *corners, x, k, inverse)


def update(child_map, mults, panel, far, base):
    span = base.shape[0]
    kids = child_map.shape[2] // 4
    blocks = span // BLK

    def kernel(map_s, top, bottom, _, far, base, updated, panel, order, done, sem):
        _, col = places()
        panel[3 * PAIR :, :] = far[...]

        def visit(t, place):
            order[place] = t

        each_block(map_s, col, blocks, kids, visit)
        for a in range(kids):
            order[blocks - kids + a] = map_s[0, 1, col * kids + a] - col * blocks

        def store(n):
            return pltpu.make_async_copy(done.at[n], updated.at[0, :, at(order[n])], sem.at[n])

        for n in range(0, blocks, TILE // BLK):
            for r in range(0, span, TILE):
                rows = slice(r, r + TILE)
                first = top.shape[0]
                part_of = top[rows, :] if r < first else bottom[r - first : r - first + TILE, :]
                total = dot(part_of, panel[:, n * BLK : n * BLK + TILE])
                for m in range(TILE // BLK):
                    part = total[:, m * BLK : (m + 1) * BLK]
                    done[n + m, rows, :] = (base[rows, at(order[n + m])] - part).astype(BF16)
            for m in range(TILE // BLK):
                store(n + m).start()
        for n in range(blocks):
            store(n).wait()

    return pl.pallas_call(
        kernel,
        out_shape=(out(1, span, span), out(*panel.shape)),
        in_specs=[SMEM] + [VMEM] * 5,
        out_specs=(HBM, VMEM),
        input_output_aliases={3: 1},
        scratch_shapes=[
            pltpu.SMEM((blocks,), jnp.int32),
            pltpu.VMEM((blocks, span, BLK), BF16),
            pltpu.SemaphoreType.DMA((blocks,)),
        ],
        compiler_params=params(14),
        cost_estimate=SMALL,
        name="update",
    )(child_map, *mults, panel, far, base)[0]


def body(front_matrix, kept_child, passed_child, child_map, pivots, pivot_inverse):
    hold = lax.optimization_barrier
    kid = kept_child.shape[1]
    arrived = flip(passed_child, "front", 1)
    u = early(child_map, pivots, front_matrix, kept_child)
    un, up = shift(u, "row", -1), shift(u, "row", 1)
    rows32, cols32 = prepare(child_map, pivots, front_matrix, kept_child)
    base = make_base(child_map, front_matrix, kept_child)
    arrived, _, rows32, cols32, base = hold((arrived, u, rows32, cols32, base))
    a, top, bottom, cross = extract(child_map, pivots, rows32, cols32, arrived)
    tfar, tnear = flip(top, "col", 2), flip(top, "col", 1)
    an, ap = shift(a, "row", -1), shift(a, "row", 1)
    cross2 = shift(cross, "row", 2)
    base = add_child(child_map, base, arrived)
    un, up, an, ap, cross2, base, tfar, tnear, bottom = hold(
        (un, up, an, ap, cross2, base, tfar, tnear, bottom)
    )
    panel, onward = stage((u, un, up), (a, an, ap))
    far = hand_on(onward)
    crosses = jnp.stack([cross, an[:BLK, kid:], cross2, ap[:BLK, kid:]])
    xfar, xnear = flip(crosses, "col", 2), flip(crosses, "col", 1)
    bfar, bnear = flip(bottom, "col", 2), flip(bottom, "col", 1)
    tcorners = [flip(tfar[n : n + TILE], "col", 1) for n in range(0, top.shape[0], TILE)]
    first, second = begin((top, tnear, tfar), tcorners, pivot_inverse)
    xfar, xnear, panel, first, second = hold((xfar, xnear, panel, first, second))
    xcorners = [flip(xfar[n : n + 2], "col", 1) for n in (0, 2)]
    upper, x, k = multiply_top((crosses, xnear, xfar, *xcorners), first, second, pivot_inverse)
    upper, bfar, bnear = hold((upper, bfar, bnear))
    bcorners = [flip(bfar[n : n + PAIR], "col", 1) for n in range(0, bottom.shape[0], PAIR)]
    lower = multiply_bottom((bottom, bnear, bfar), bcorners, x, k, pivot_inverse)
    lower, far = hold((lower, far))
    return update(child_map, (upper, lower), panel, far, base)


def solution(mesh):
    in_specs = (
        P("front", "row", "col"),
        P("front", "row", "col"),
        P("front", "row", "col"),
        P("front", None, None),
        P("front", None, None),
        P("front", None, None, None),
    )
    out_specs = P("front", "row", "col")
    return jax.shard_map(body, mesh=mesh, in_specs=in_specs, out_specs=out_specs, check_vma=False)
```

```python
import jax
import jax.numpy as jnp
from jax import lax
from jax.experimental import pallas as pl
from jax.experimental.pallas import tpu as pltpu
from jax.sharding import PartitionSpec as P

BLK = 128
PAIR = 2 * BLK
TILE = 512
P_SIZE = 512
F32 = jnp.float32
BF16 = jnp.bfloat16
VMEM = pl.BlockSpec(memory_space=pltpu.VMEM)
HBM = pl.BlockSpec(memory_space=pltpu.HBM)
SMEM = pl.BlockSpec(memory_space=pltpu.SMEM)
MIB = 1 << 20
SMALL = pl.CostEstimate(flops=1000, bytes_accessed=1000, transcendentals=0)


def shift(x, axis, step):
    n = lax.axis_size(axis)
    return lax.ppermute(x, axis, [(i, (i + step) % n) for i in range(n)])


def flip(x, axis, bit):
    n = lax.axis_size(axis)
    return lax.ppermute(x, axis, [(i, i ^ bit) for i in range(n)])


def at(block, size=BLK):
    return pl.ds(pl.multiple_of(block * size, size), size)


def places():
    return lax.axis_index("row"), lax.axis_index("col")


def dot(a, b):
    return jnp.dot(a, b, preferred_element_type=F32)


def dot_t(a, b):
    return lax.dot_general(a, b, (((1,), (1,)), ((), ())), preferred_element_type=F32)


def out(*shape, dtype=BF16):
    return jax.ShapeDtypeStruct(shape, dtype)


def params(mib):
    return pltpu.CompilerParams(vmem_limit_bytes=mib * MIB)


def add_rows(acc, child, which, s, map_s, piv_s, row, col, here, kids):
    for k in range(kids):

        @pl.when(map_s[0, which, row * kids + k] == piv_s[0, s, row])
        def _():
            for a in range(kids):
                t = map_s[0, which, col * kids + a] - col * here
                acc[s, :, at(t)] += child[0, k * BLK : (k + 1) * BLK, a * BLK : (a + 1) * BLK].astype(F32)


def add_cols(acc, child, which, s, map_s, piv_s, row, col, here, kids):
    for k in range(kids):

        @pl.when(map_s[0, which, col * kids + k] == piv_s[0, s, col])
        def _():
            for a in range(kids):
                t = map_s[0, which, row * kids + a] - row * here
                acc[s, at(t), :] += child[0, a * BLK : (a + 1) * BLK, k * BLK : (k + 1) * BLK].astype(F32)


def scalars(map_ref, piv_ref, map_s, piv_s, sem):
    first = pltpu.make_async_copy(map_ref, map_s, sem.at[0])
    second = pltpu.make_async_copy(piv_ref, piv_s, sem.at[1])
    first.start()
    second.start()
    first.wait()
    second.wait()


def each_block(map_s, col, here, kids, visit):
    place = jnp.int32(0)
    for t in range(here):
        hit = jnp.bool_(False)
        for a in range(kids):
            hit = hit | (map_s[0, 1, col * kids + a] - col * here == t)

        @pl.when(jnp.logical_not(hit))
        def _():
            visit(t, place)

        place = place + jnp.where(hit, 0, 1)


def early_kernel(map_ref, piv_ref, front, kept, rows_out, map_s, piv_s, rows_in, kid, sem):
    row, col = places()
    here = front.shape[1] // BLK
    kids = kept.shape[1] // BLK
    child = pltpu.make_async_copy(kept, kid, sem.at[2])
    child.start()
    scalars(map_ref, piv_ref, map_s, piv_s, sem)
    copies = []
    for s in range(2):
        pr = piv_s[0, s, row] - row * here
        copies.append(pltpu.make_async_copy(front.at[0, at(pr), :], rows_in.at[s], sem.at[s]))
    for c in copies:
        c.start()
    for c in copies:
        c.wait()
    child.wait()
    for s in range(2):
        for k in range(kids):

            @pl.when(map_s[0, 0, row * kids + k] == piv_s[0, s, row])
            def _():
                for a in range(kids):
                    t = at(map_s[0, 0, col * kids + a] - col * here)
                    piece = kid[0, k * BLK : (k + 1) * BLK, a * BLK : (a + 1) * BLK].astype(F32)
                    rows_in[s, :, t] = (rows_in[s, :, t].astype(F32) + piece).astype(BF16)

    def visit(t, place):
        for s in range(2):
            rows_out[s * BLK : (s + 1) * BLK, at(place)] = rows_in[s, :, t * BLK : (t + 1) * BLK]

    each_block(map_s, col, here, kids, visit)


def early(child_map, pivots, front, kept):
    span = front.shape[1]
    return pl.pallas_call(
        early_kernel,
        out_shape=out(PAIR, span - kept.shape[1]),
        in_specs=[HBM] * 4,
        out_specs=VMEM,
        scratch_shapes=[
            pltpu.SMEM(child_map.shape, jnp.int32),
            pltpu.SMEM(pivots.shape, jnp.int32),
            pltpu.VMEM((2, BLK, span), BF16),
            pltpu.VMEM(kept.shape, BF16),
            pltpu.SemaphoreType.DMA((3,)),
        ],
        compiler_params=params(57),
        cost_estimate=SMALL,
        name="early",
    )(child_map, pivots, front, kept)


def prepare_kernel(
    map_ref, piv_ref, front, kept, rows_out, cols32, map_s, piv_s, rows_in, cols_in, rows32, sem
):
    row, col = places()
    here = front.shape[1] // BLK
    kids = kept.shape[1] // BLK
    scalars(map_ref, piv_ref, map_s, piv_s, sem)
    copies = []
    for s in range(2):
        pr = piv_s[0, s, row] - row * here
        pc = piv_s[0, s, col] - col * here
        copies.append(pltpu.make_async_copy(front.at[0, at(pr), :], rows_in.at[s], sem.at[2 * s]))
        copies.append(pltpu.make_async_copy(front.at[0, :, at(pc)], cols_in.at[s], sem.at[2 * s + 1]))
    for c in copies:
        c.start()
    for c in copies:
        c.wait()
    rows32[...] = rows_in[...].astype(F32)
    cols32[...] = cols_in[...].astype(F32)
    for s in range(2):
        add_rows(rows32, kept, 0, s, map_s, piv_s, row, col, here, kids)
        add_cols(cols32, kept, 0, s, map_s, piv_s, row, col, here, kids)
        for a in range(kids):
            t = map_s[0, 1, col * kids + a] - col * here
            rows_out[s, :, a * BLK : (a + 1) * BLK] = rows32[s, :, at(t)]


def prepare(child_map, pivots, front, kept):
    span = front.shape[1]
    return pl.pallas_call(
        prepare_kernel,
        out_shape=(out(2, BLK, kept.shape[1], dtype=F32), out(2, span, BLK, dtype=F32)),
        in_specs=[HBM, HBM, HBM, VMEM],
        out_specs=(VMEM, VMEM),
        scratch_shapes=[
            pltpu.SMEM(child_map.shape, jnp.int32),
            pltpu.SMEM(pivots.shape, jnp.int32),
            pltpu.VMEM((2, BLK, span), BF16),
            pltpu.VMEM((2, span, BLK), BF16),
            pltpu.VMEM((2, BLK, span), F32),
            pltpu.SemaphoreType.DMA((4,)),
        ],
        compiler_params=params(12),
        cost_estimate=SMALL,
        name="prepare",
    )(child_map, pivots, front, kept)


def extract_kernel(map_s, piv_s, rows32, cols32, arrived, rows_out, top, bottom, cross, cols):
    row, col = places()
    here = cols.shape[0] // BLK
    kids = arrived.shape[1] // BLK
    for s in range(2):
        own = slice(s * BLK, (s + 1) * BLK)
        rows_out[own, : kids * BLK] = rows32[s].astype(BF16)
        cols[:, own] = cols32[s].astype(BF16)
        for k in range(kids):

            @pl.when(map_s[0, 1, row * kids + k] == piv_s[0, s, row])
            def _():
                piece = arrived[0, k * BLK : (k + 1) * BLK, :].astype(F32)
                rows_out[own, : kids * BLK] = (rows32[s] + piece).astype(BF16)

            @pl.when(map_s[0, 1, col * kids + k] == piv_s[0, s, col])
            def _():
                for a in range(kids):
                    t = map_s[0, 1, row * kids + a] - row * here
                    piece = arrived[0, a * BLK : (a + 1) * BLK, k * BLK : (k + 1) * BLK].astype(F32)
                    cols[at(t), own] = (cols32[s, at(t), :] + piece).astype(BF16)

    top[...] = cols[: top.shape[0], :]
    bottom[...] = cols[top.shape[0] :, :]
    block = cols[at(piv_s[0, 1, row] - row * here), :BLK]
    rows_out[:BLK, kids * BLK :] = block
    rows_out[BLK:, kids * BLK :] = jnp.zeros((BLK, BLK), BF16)
    cross[...] = block


def extract(child_map, pivots, rows32, cols32, arrived):
    span = cols32.shape[1]
    return pl.pallas_call(
        extract_kernel,
        out_shape=(
            out(PAIR, arrived.shape[1] + BLK),
            out(span - TILE, PAIR),
            out(TILE, PAIR),
            out(BLK, BLK),
        ),
        in_specs=[SMEM] * 2 + [VMEM] * 3,
        out_specs=(VMEM,) * 4,
        scratch_shapes=[pltpu.VMEM((span, PAIR), BF16)],
        compiler_params=params(8),
        cost_estimate=SMALL,
        name="extract",
    )(child_map, pivots, rows32, cols32, arrived)


def add_blocks(base, child, which, map_s, first, deep):
    row, col = places()
    here = base.shape[1] // BLK
    kids = child.shape[1] // BLK
    for k in range(kids):
        t = map_s[0, which, row * kids + k] - row * here

        @pl.when((t >= first) & (t < first + deep))
        def _():
            for a in range(kids):
                u = map_s[0, which, col * kids + a] - col * here
                piece = child[0, k * BLK : (k + 1) * BLK, a * BLK : (a + 1) * BLK]
                base[at(t), at(u)] += piece.astype(F32)


def make_base(child_map, front, kept):
    span = front.shape[1]
    steps = 4
    width = span // steps

    def kernel(map_s, front, kept, base):
        step = pl.program_id(0)
        base[at(step, width), :] = front[0].astype(F32)
        add_blocks(base, kept, 0, map_s, step * (width // BLK), width // BLK)

    return pl.pallas_call(
        kernel,
        grid=(steps,),
        out_shape=out(span, span, dtype=F32),
        in_specs=[SMEM, pl.BlockSpec((1, width, span), lambda i: (0, i, 0)), VMEM],
        out_specs=VMEM,
        compiler_params=params(14),
        cost_estimate=SMALL,
        name="base",
    )(child_map, front, kept)


def add_child(child_map, base, arrived):
    def kernel(map_s, _, arrived, base):
        add_blocks(base, arrived, 1, map_s, 0, base.shape[0] // BLK)

    return pl.pallas_call(
        kernel,
        out_shape=out(*base.shape, dtype=F32),
        in_specs=[SMEM, VMEM, VMEM],
        out_specs=VMEM,
        input_output_aliases={1: 0},
        compiler_params=params(4),
        cost_estimate=SMALL,
        name="add_child",
    )(child_map, base, arrived)


def stage(us, as_):
    split = us[0].shape[1]
    kid = as_[0].shape[1] - BLK

    def kernel(u0, u1, u2, a0, a1, a2, panel, onward):
        _, col = places()
        even = lax.rem(col, 2) == 0
        for n, (u, a) in enumerate(((u0, a0), (u1, a1), (u2, a2))):
            panel[n * PAIR : (n + 1) * PAIR, :split] = u[...]
            panel[n * PAIR : (n + 1) * PAIR, split:] = a[:, :kid]

        @pl.when(even)
        def _():
            onward[:, :split] = u2[...]
            onward[:, split:] = a2[:, :kid]

        @pl.when(jnp.logical_not(even))
        def _():
            onward[:, :split] = u1[...]
            onward[:, split:] = a1[:, :kid]

    return pl.pallas_call(
        kernel,
        out_shape=(out(2 * P_SIZE, split + kid), out(PAIR, split + kid)),
        in_specs=[VMEM] * 6,
        out_specs=(VMEM, VMEM),
        compiler_params=params(4),
        cost_estimate=SMALL,
        name="stage",
    )(*us, *as_)


def hand_on(x):
    rows, cols = lax.axis_size("row"), lax.axis_size("col")
    route = []
    for r in range(rows):
        for c in range(cols):
            to = (r + 1) % rows if c % 2 == 0 else (r - 1) % rows
            route.append((r * cols + c, to * cols + c))
    return lax.ppermute(x, ("row", "col"), route)


def begin(pieces, corners, inverse):
    span = pieces[0].shape[0]

    def kernel(c0, c1, c2, *rest):
        *corners, inverse, first, second = rest
        _, col = places()
        js = [lax.bitwise_xor(col, q) for q in range(4)]
        for n, corner in enumerate(corners):
            rows = slice(n * PAIR, (n + 1) * PAIR)
            total = dot(corner[:, :BLK], inverse[0, 0, at(js[3]), :])
            second[rows, at(js[3])] = corner[:, BLK:]
            for q, c in enumerate((c0, c1, c2)):
                total += dot(c[rows, :BLK], inverse[0, 0, at(js[q]), :])
                second[rows, at(js[q])] = c[rows, BLK:]
            first[rows, :] = total

    return pl.pallas_call(
        kernel,
        out_shape=(out(span, P_SIZE, dtype=F32), out(span, P_SIZE)),
        in_specs=[VMEM] * (4 + len(corners)),
        out_specs=(VMEM, VMEM),
        compiler_params=params(6),
        cost_estimate=SMALL,
        name="begin",
    )(*pieces, *corners, inverse)


def ring_places(row):
    found = []
    for j in range(4):
        d = lax.rem(j - row + 4, 4)
        found.append(jnp.where(d < 2, d, 5 - d))
    return found


def eliminate(mult, rows, m1, i2, x, k, inverse, place):
    p2 = (i2.astype(F32) - dot_t(m1.astype(BF16), x[...])).astype(BF16)
    m2 = dot(p2, inverse[0, 1]).astype(BF16)
    n1 = (m1 - dot_t(m2, k[...])).astype(BF16)
    for j in range(4):
        b = slice(j * BLK, (j + 1) * BLK)
        mult[rows, at(2 * place[j])] = n1[:, b]
        mult[rows, at(2 * place[j] + 1)] = m2[:, b]


def multiply_top(crosses, first, second, inverse):
    span = first.shape[0]

    def kernel(x0, x1, x2, x3, x4, first, second, inverse, mult, x, k):
        row, col = places()
        for q, xq in enumerate((x0, x1, x2, (x3, x4))):
            j = lax.bitwise_xor(col, q)
            for d in range(4):
                x[at(lax.rem(row + d, 4)), at(j)] = xq[d // 2][d % 2] if q == 3 else xq[d]
        k[...] = dot_t(inverse[0, 0], x[...]).astype(BF16)
        place = ring_places(row)
        for r in range(0, span, TILE):
            rows = slice(r, r + TILE)
            eliminate(mult, rows, first[rows, :], second[rows, :], x, k, inverse, place)

    return pl.pallas_call(
        kernel,
        out_shape=(out(span, 2 * P_SIZE), out(P_SIZE, P_SIZE), out(P_SIZE, P_SIZE)),
        in_specs=[VMEM] * 8,
        out_specs=(VMEM,) * 3,
        compiler_params=params(8),
        cost_estimate=SMALL,
        name="multiply_top",
    )(*crosses, first, second, inverse)


def multiply_bottom(pieces, corners, x, k, inverse):
    span = pieces[0].shape[0]

    def kernel(c0, c1, c2, k0, k1, x, k, inverse, mult, p1, i2):
        row, col = places()
        for q, c in enumerate((c0, c1, c2)):
            j = lax.bitwise_xor(col, q)
            p1[:, at(j)] = c[:, :BLK]
            i2[:, at(j)] = c[:, BLK:]
        j = lax.bitwise_xor(col, 3)
        for n, corner in enumerate((k0, k1)):
            rows = slice(n * PAIR, (n + 1) * PAIR)
            p1[rows, at(j)] = corner[:, :BLK]
            i2[rows, at(j)] = corner[:, BLK:]
        m1 = dot(p1[...], inverse[0, 0])
        eliminate(mult, slice(0, span), m1, i2[...], x, k, inverse, ring_places(row))

    return pl.pallas_call(
        kernel,
        out_shape=out(span, 2 * P_SIZE),
        in_specs=[VMEM] * 8,
        out_specs=VMEM,
        scratch_shapes=[pltpu.VMEM((span, P_SIZE), BF16)] * 2,
        compiler_params=params(8),
        cost_estimate=SMALL,
        name="multiply_bottom",
    )(*pieces, *corners, x, k, inverse)


def update(child_map, mults, panel, far, base):
    span = base.shape[0]
    kids = child_map.shape[2] // 4
    blocks = span // BLK

    def kernel(map_s, top, bottom, _, far, base, updated, panel, order, done, sem):
        _, col = places()
        panel[3 * PAIR :, :] = far[...]

        def visit(t, place):
            order[place] = t

        each_block(map_s, col, blocks, kids, visit)
        for a in range(kids):
            order[blocks - kids + a] = map_s[0, 1, col * kids + a] - col * blocks

        def store(n):
            return pltpu.make_async_copy(done.at[n], updated.at[0, :, at(order[n])], sem.at[n])

        n = 0
        while n < blocks:
            count = TILE // BLK if blocks - n > TILE // BLK else 2
            for r in range(0, span, TILE):
                rows = slice(r, r + TILE)
                first = top.shape[0]
                part_of = top[rows, :] if r < first else bottom[r - first : r - first + TILE, :]
                total = dot(part_of, panel[:, n * BLK : (n + count) * BLK])
                for m in range(count):
                    part = total[:, m * BLK : (m + 1) * BLK]
                    done[n + m, rows, :] = (base[rows, at(order[n + m])] - part).astype(BF16)
            for m in range(count):
                store(n + m).start()
            n += count
        for n in range(blocks):
            store(n).wait()

    return pl.pallas_call(
        kernel,
        out_shape=(out(1, span, span), out(*panel.shape)),
        in_specs=[SMEM] + [VMEM] * 5,
        out_specs=(HBM, VMEM),
        input_output_aliases={3: 1},
        scratch_shapes=[
            pltpu.SMEM((blocks,), jnp.int32),
            pltpu.VMEM((blocks, span, BLK), BF16),
            pltpu.SemaphoreType.DMA((blocks,)),
        ],
        compiler_params=params(14),
        cost_estimate=SMALL,
        name="update",
    )(child_map, *mults, panel, far, base)[0]


def body(front_matrix, kept_child, passed_child, child_map, pivots, pivot_inverse):
    hold = lax.optimization_barrier
    kid = kept_child.shape[1]
    arrived = flip(passed_child, "front", 1)
    u = early(child_map, pivots, front_matrix, kept_child)
    un, up = shift(u, "row", -1), shift(u, "row", 1)
    rows32, cols32 = prepare(child_map, pivots, front_matrix, kept_child)
    base = make_base(child_map, front_matrix, kept_child)
    arrived, _, rows32, cols32, base = hold((arrived, u, rows32, cols32, base))
    a, top, bottom, cross = extract(child_map, pivots, rows32, cols32, arrived)
    tfar, tnear = flip(top, "col", 2), flip(top, "col", 1)
    an, ap = shift(a, "row", -1), shift(a, "row", 1)
    cross2 = shift(cross, "row", 2)
    base = add_child(child_map, base, arrived)
    un, up, an, ap, cross2, base, tfar, tnear, bottom = hold(
        (un, up, an, ap, cross2, base, tfar, tnear, bottom)
    )
    panel, onward = stage((u, un, up), (a, an, ap))
    far = hand_on(onward)
    crosses = jnp.stack([cross, an[:BLK, kid:], cross2, ap[:BLK, kid:]])
    xfar, xnear = flip(crosses, "col", 2), flip(crosses, "col", 1)
    bfar, bnear = flip(bottom, "col", 2), flip(bottom, "col", 1)
    tcorners = [flip(tfar[n : n + PAIR], "col", 1) for n in range(0, top.shape[0], PAIR)]
    xfar, xnear, panel = hold((xfar, xnear, panel))
    xcorners = [flip(xfar[n : n + 2], "col", 1) for n in (0, 2)]
    first, second = begin((top, tnear, tfar), tcorners, pivot_inverse)
    first, second, xcorners = hold((first, second, xcorners))
    upper, x, k = multiply_top((crosses, xnear, xfar, *xcorners), first, second, pivot_inverse)
    upper, bfar, bnear = hold((upper, bfar, bnear))
    bcorners = [flip(bfar[n : n + PAIR], "col", 1) for n in range(0, bottom.shape[0], PAIR)]
    lower = multiply_bottom((bottom, bnear, bfar), bcorners, x, k, pivot_inverse)
    lower, far = hold((lower, far))
    return update(child_map, (upper, lower), panel, far, base)


def solution(mesh):
    in_specs = (
        P("front", "row", "col"),
        P("front", "row", "col"),
        P("front", "row", "col"),
        P("front", None, None),
        P("front", None, None),
        P("front", None, None, None),
    )
    out_specs = P("front", "row", "col")
    return jax.shard_map(body, mesh=mesh, in_specs=in_specs, out_specs=out_specs, check_vma=False)
```

```python
import jax
import jax.numpy as jnp
from jax import lax
from jax.experimental import pallas as pl
from jax.experimental.pallas import tpu as pltpu
from jax.sharding import PartitionSpec as P

BLK = 128
PAIR = 2 * BLK
TILE = 512
P_SIZE = 512
F32 = jnp.float32
BF16 = jnp.bfloat16
VMEM = pl.BlockSpec(memory_space=pltpu.VMEM)
HBM = pl.BlockSpec(memory_space=pltpu.HBM)
SMEM = pl.BlockSpec(memory_space=pltpu.SMEM)
MIB = 1 << 20
SMALL = pl.CostEstimate(flops=1000, bytes_accessed=1000, transcendentals=0)


def shift(x, axis, step):
    n = lax.axis_size(axis)
    return lax.ppermute(x, axis, [(i, (i + step) % n) for i in range(n)])


def flip(x, axis, bit):
    n = lax.axis_size(axis)
    return lax.ppermute(x, axis, [(i, i ^ bit) for i in range(n)])


def at(block, size=BLK):
    return pl.ds(pl.multiple_of(block * size, size), size)


def places():
    return lax.axis_index("row"), lax.axis_index("col")


def dot(a, b):
    return jnp.dot(a, b, preferred_element_type=F32)


def dot_t(a, b):
    return lax.dot_general(a, b, (((1,), (1,)), ((), ())), preferred_element_type=F32)


def out(*shape, dtype=BF16):
    return jax.ShapeDtypeStruct(shape, dtype)


def params(mib):
    return pltpu.CompilerParams(vmem_limit_bytes=mib * MIB)


def add_rows(acc, child, which, s, map_s, piv_s, row, col, here, kids):
    for k in range(kids):

        @pl.when(map_s[0, which, row * kids + k] == piv_s[0, s, row])
        def _():
            for a in range(kids):
                t = map_s[0, which, col * kids + a] - col * here
                acc[s, :, at(t)] += child[0, k * BLK : (k + 1) * BLK, a * BLK : (a + 1) * BLK].astype(F32)


def add_cols(acc, child, which, s, map_s, piv_s, row, col, here, kids):
    for k in range(kids):

        @pl.when(map_s[0, which, col * kids + k] == piv_s[0, s, col])
        def _():
            for a in range(kids):
                t = map_s[0, which, row * kids + a] - row * here
                acc[s, at(t), :] += child[0, a * BLK : (a + 1) * BLK, k * BLK : (k + 1) * BLK].astype(F32)


def scalars(map_ref, piv_ref, map_s, piv_s, sem):
    first = pltpu.make_async_copy(map_ref, map_s, sem.at[0])
    second = pltpu.make_async_copy(piv_ref, piv_s, sem.at[1])
    first.start()
    second.start()
    first.wait()
    second.wait()


def each_block(map_s, col, here, kids, visit):
    place = jnp.int32(0)
    for t in range(here):
        hit = jnp.bool_(False)
        for a in range(kids):
            hit = hit | (map_s[0, 1, col * kids + a] - col * here == t)

        @pl.when(jnp.logical_not(hit))
        def _():
            visit(t, place)

        place = place + jnp.where(hit, 0, 1)


def early_kernel(map_ref, piv_ref, front, kept, rows_out, map_s, piv_s, rows_in, kid, sem):
    row, col = places()
    here = front.shape[1] // BLK
    kids = kept.shape[1] // BLK
    child = pltpu.make_async_copy(kept, kid, sem.at[2])
    child.start()
    scalars(map_ref, piv_ref, map_s, piv_s, sem)
    copies = []
    for s in range(2):
        pr = piv_s[0, s, row] - row * here
        copies.append(pltpu.make_async_copy(front.at[0, at(pr), :], rows_in.at[s], sem.at[s]))
    for c in copies:
        c.start()
    for c in copies:
        c.wait()
    child.wait()
    for s in range(2):
        for k in range(kids):

            @pl.when(map_s[0, 0, row * kids + k] == piv_s[0, s, row])
            def _():
                for a in range(kids):
                    t = at(map_s[0, 0, col * kids + a] - col * here)
                    piece = kid[0, k * BLK : (k + 1) * BLK, a * BLK : (a + 1) * BLK].astype(F32)
                    rows_in[s, :, t] = (rows_in[s, :, t].astype(F32) + piece).astype(BF16)

    def visit(t, place):
        for s in range(2):
            rows_out[s * BLK : (s + 1) * BLK, at(place)] = rows_in[s, :, t * BLK : (t + 1) * BLK]

    each_block(map_s, col, here, kids, visit)


def early(child_map, pivots, front, kept):
    span = front.shape[1]
    return pl.pallas_call(
        early_kernel,
        out_shape=out(PAIR, span - kept.shape[1]),
        in_specs=[HBM] * 4,
        out_specs=VMEM,
        scratch_shapes=[
            pltpu.SMEM(child_map.shape, jnp.int32),
            pltpu.SMEM(pivots.shape, jnp.int32),
            pltpu.VMEM((2, BLK, span), BF16),
            pltpu.VMEM(kept.shape, BF16),
            pltpu.SemaphoreType.DMA((3,)),
        ],
        compiler_params=params(57),
        cost_estimate=SMALL,
        name="early",
    )(child_map, pivots, front, kept)


def prepare_kernel(
    map_ref, piv_ref, front, kept, rows_out, cols32, map_s, piv_s, rows_in, cols_in, rows32, sem
):
    row, col = places()
    here = front.shape[1] // BLK
    kids = kept.shape[1] // BLK
    scalars(map_ref, piv_ref, map_s, piv_s, sem)
    copies = []
    for s in range(2):
        pr = piv_s[0, s, row] - row * here
        pc = piv_s[0, s, col] - col * here
        copies.append(pltpu.make_async_copy(front.at[0, at(pr), :], rows_in.at[s], sem.at[2 * s]))
        copies.append(pltpu.make_async_copy(front.at[0, :, at(pc)], cols_in.at[s], sem.at[2 * s + 1]))
    for c in copies:
        c.start()
    for c in copies:
        c.wait()
    rows32[...] = rows_in[...].astype(F32)
    cols32[...] = cols_in[...].astype(F32)
    for s in range(2):
        add_rows(rows32, kept, 0, s, map_s, piv_s, row, col, here, kids)
        add_cols(cols32, kept, 0, s, map_s, piv_s, row, col, here, kids)
        for a in range(kids):
            t = map_s[0, 1, col * kids + a] - col * here
            rows_out[s, :, a * BLK : (a + 1) * BLK] = rows32[s, :, at(t)]


def prepare(child_map, pivots, front, kept):
    span = front.shape[1]
    return pl.pallas_call(
        prepare_kernel,
        out_shape=(out(2, BLK, kept.shape[1], dtype=F32), out(2, span, BLK, dtype=F32)),
        in_specs=[HBM, HBM, HBM, VMEM],
        out_specs=(VMEM, VMEM),
        scratch_shapes=[
            pltpu.SMEM(child_map.shape, jnp.int32),
            pltpu.SMEM(pivots.shape, jnp.int32),
            pltpu.VMEM((2, BLK, span), BF16),
            pltpu.VMEM((2, span, BLK), BF16),
            pltpu.VMEM((2, BLK, span), F32),
            pltpu.SemaphoreType.DMA((4,)),
        ],
        compiler_params=params(12),
        cost_estimate=SMALL,
        name="prepare",
    )(child_map, pivots, front, kept)


def extract_kernel(map_s, piv_s, rows32, cols32, arrived, rows_out, top, bottom, cross, cols):
    row, col = places()
    here = cols.shape[0] // BLK
    kids = arrived.shape[1] // BLK
    for s in range(2):
        own = slice(s * BLK, (s + 1) * BLK)
        rows_out[own, : kids * BLK] = rows32[s].astype(BF16)
        cols[:, own] = cols32[s].astype(BF16)
        for k in range(kids):

            @pl.when(map_s[0, 1, row * kids + k] == piv_s[0, s, row])
            def _():
                piece = arrived[0, k * BLK : (k + 1) * BLK, :].astype(F32)
                rows_out[own, : kids * BLK] = (rows32[s] + piece).astype(BF16)

            @pl.when(map_s[0, 1, col * kids + k] == piv_s[0, s, col])
            def _():
                for a in range(kids):
                    t = map_s[0, 1, row * kids + a] - row * here
                    piece = arrived[0, a * BLK : (a + 1) * BLK, k * BLK : (k + 1) * BLK].astype(F32)
                    cols[at(t), own] = (cols32[s, at(t), :] + piece).astype(BF16)

    top[...] = cols[: top.shape[0], :]
    bottom[...] = cols[top.shape[0] :, :]
    block = cols[at(piv_s[0, 1, row] - row * here), :BLK]
    rows_out[:BLK, kids * BLK :] = block
    rows_out[BLK:, kids * BLK :] = jnp.zeros((BLK, BLK), BF16)
    cross[...] = block


def extract(child_map, pivots, rows32, cols32, arrived):
    span = cols32.shape[1]
    return pl.pallas_call(
        extract_kernel,
        out_shape=(
            out(PAIR, arrived.shape[1] + BLK),
            out(span - TILE, PAIR),
            out(TILE, PAIR),
            out(BLK, BLK),
        ),
        in_specs=[SMEM] * 2 + [VMEM] * 3,
        out_specs=(VMEM,) * 4,
        scratch_shapes=[pltpu.VMEM((span, PAIR), BF16)],
        compiler_params=params(8),
        cost_estimate=SMALL,
        name="extract",
    )(child_map, pivots, rows32, cols32, arrived)


def add_blocks(base, child, which, map_s, first, deep):
    row, col = places()
    here = base.shape[1] // BLK
    kids = child.shape[1] // BLK
    for k in range(kids):
        t = map_s[0, which, row * kids + k] - row * here

        @pl.when((t >= first) & (t < first + deep))
        def _():
            for a in range(kids):
                u = map_s[0, which, col * kids + a] - col * here
                piece = child[0, k * BLK : (k + 1) * BLK, a * BLK : (a + 1) * BLK]
                base[at(t), at(u)] += piece.astype(F32)


def make_base(child_map, front, kept):
    span = front.shape[1]
    steps = 4
    width = span // steps

    def kernel(map_s, front, kept, base):
        step = pl.program_id(0)
        base[at(step, width), :] = front[0].astype(F32)
        add_blocks(base, kept, 0, map_s, step * (width // BLK), width // BLK)

    return pl.pallas_call(
        kernel,
        grid=(steps,),
        out_shape=out(span, span, dtype=F32),
        in_specs=[SMEM, pl.BlockSpec((1, width, span), lambda i: (0, i, 0)), VMEM],
        out_specs=VMEM,
        compiler_params=params(14),
        cost_estimate=SMALL,
        name="base",
    )(child_map, front, kept)


def add_child(child_map, base, arrived):
    def kernel(map_s, _, arrived, base):
        add_blocks(base, arrived, 1, map_s, 0, base.shape[0] // BLK)

    return pl.pallas_call(
        kernel,
        out_shape=out(*base.shape, dtype=F32),
        in_specs=[SMEM, VMEM, VMEM],
        out_specs=VMEM,
        input_output_aliases={1: 0},
        compiler_params=params(4),
        cost_estimate=SMALL,
        name="add_child",
    )(child_map, base, arrived)


def stage(us, as_):
    split = us[0].shape[1]
    kid = as_[0].shape[1] - BLK

    def kernel(u0, u1, u2, a0, a1, a2, panel, onward):
        _, col = places()
        even = lax.rem(col, 2) == 0
        for n, (u, a) in enumerate(((u0, a0), (u1, a1), (u2, a2))):
            panel[n * PAIR : (n + 1) * PAIR, :split] = u[...]
            panel[n * PAIR : (n + 1) * PAIR, split:] = a[:, :kid]

        @pl.when(even)
        def _():
            onward[:, :split] = u2[...]
            onward[:, split:] = a2[:, :kid]

        @pl.when(jnp.logical_not(even))
        def _():
            onward[:, :split] = u1[...]
            onward[:, split:] = a1[:, :kid]

    return pl.pallas_call(
        kernel,
        out_shape=(out(2 * P_SIZE, split + kid), out(PAIR, split + kid)),
        in_specs=[VMEM] * 6,
        out_specs=(VMEM, VMEM),
        compiler_params=params(4),
        cost_estimate=SMALL,
        name="stage",
    )(*us, *as_)


def hand_on(x):
    rows, cols = lax.axis_size("row"), lax.axis_size("col")
    route = []
    for r in range(rows):
        for c in range(cols):
            to = (r + 1) % rows if c % 2 == 0 else (r - 1) % rows
            route.append((r * cols + c, to * cols + c))
    return lax.ppermute(x, ("row", "col"), route)


def begin(pieces, corners, inverse):
    span = pieces[0].shape[0]

    def kernel(c0, c1, c2, *rest):
        *corners, inverse, first, second = rest
        _, col = places()
        js = [lax.bitwise_xor(col, q) for q in range(4)]
        for n, corner in enumerate(corners):
            rows = slice(n * PAIR, (n + 1) * PAIR)
            total = dot(corner[:, :BLK], inverse[0, 0, at(js[3]), :])
            second[rows, at(js[3])] = corner[:, BLK:]
            for q, c in enumerate((c0, c1, c2)):
                total += dot(c[rows, :BLK], inverse[0, 0, at(js[q]), :])
                second[rows, at(js[q])] = c[rows, BLK:]
            first[rows, :] = total

    return pl.pallas_call(
        kernel,
        out_shape=(out(span, P_SIZE, dtype=F32), out(span, P_SIZE)),
        in_specs=[VMEM] * (4 + len(corners)),
        out_specs=(VMEM, VMEM),
        compiler_params=params(6),
        cost_estimate=SMALL,
        name="begin",
    )(*pieces, *corners, inverse)


def ring_places(row):
    found = []
    for j in range(4):
        d = lax.rem(j - row + 4, 4)
        found.append(jnp.where(d < 2, d, 5 - d))
    return found


def eliminate(mult, rows, m1, i2, x, k, inverse, place):
    p2 = (i2.astype(F32) - dot_t(m1.astype(BF16), x[...])).astype(BF16)
    m2 = dot(p2, inverse[0, 1]).astype(BF16)
    n1 = (m1 - dot_t(m2, k[...])).astype(BF16)
    for j in range(4):
        b = slice(j * BLK, (j + 1) * BLK)
        mult[rows, at(2 * place[j])] = n1[:, b]
        mult[rows, at(2 * place[j] + 1)] = m2[:, b]


def multiply_top(crosses, first, second, inverse):
    span = first.shape[0]

    def kernel(x0, x1, x2, x3, x4, first, second, inverse, mult, x, k):
        row, col = places()
        for q, xq in enumerate((x0, x1, x2, (x3, x4))):
            j = lax.bitwise_xor(col, q)
            for d in range(4):
                x[at(lax.rem(row + d, 4)), at(j)] = xq[d // 2][d % 2] if q == 3 else xq[d]
        k[...] = dot_t(inverse[0, 0], x[...]).astype(BF16)
        place = ring_places(row)
        for r in range(0, span, TILE):
            rows = slice(r, r + TILE)
            eliminate(mult, rows, first[rows, :], second[rows, :], x, k, inverse, place)

    return pl.pallas_call(
        kernel,
        out_shape=(out(span, 2 * P_SIZE), out(P_SIZE, P_SIZE), out(P_SIZE, P_SIZE)),
        in_specs=[VMEM] * 8,
        out_specs=(VMEM,) * 3,
        compiler_params=params(8),
        cost_estimate=SMALL,
        name="multiply_top",
    )(*crosses, first, second, inverse)


def multiply_bottom(pieces, corners, x, k, inverse):
    span = pieces[0].shape[0]

    def kernel(c0, c1, c2, *rest):
        *corners, x, k, inverse, mult, p1, i2 = rest
        row, col = places()
        for q, c in enumerate((c0, c1, c2)):
            j = lax.bitwise_xor(col, q)
            p1[:, at(j)] = c[:, :BLK]
            i2[:, at(j)] = c[:, BLK:]
        j = lax.bitwise_xor(col, 3)
        for n, corner in enumerate(corners):
            rows = slice(n * BLK, (n + 1) * BLK)
            p1[rows, at(j)] = corner[:, :BLK]
            i2[rows, at(j)] = corner[:, BLK:]
        m1 = dot(p1[...], inverse[0, 0])
        eliminate(mult, slice(0, span), m1, i2[...], x, k, inverse, ring_places(row))

    return pl.pallas_call(
        kernel,
        out_shape=out(span, 2 * P_SIZE),
        in_specs=[VMEM] * (6 + len(corners)),
        out_specs=VMEM,
        scratch_shapes=[pltpu.VMEM((span, P_SIZE), BF16)] * 2,
        compiler_params=params(8),
        cost_estimate=SMALL,
        name="multiply_bottom",
    )(*pieces, *corners, x, k, inverse)


def update(child_map, mults, panel, far, base):
    span = base.shape[0]
    kids = child_map.shape[2] // 4
    blocks = span // BLK

    def kernel(map_s, top, bottom, _, far, base, updated, panel, order, done, sem):
        _, col = places()
        panel[3 * PAIR :, :] = far[...]

        def visit(t, place):
            order[place] = t

        each_block(map_s, col, blocks, kids, visit)
        for a in range(kids):
            order[blocks - kids + a] = map_s[0, 1, col * kids + a] - col * blocks

        def store(n):
            return pltpu.make_async_copy(done.at[n], updated.at[0, :, at(order[n])], sem.at[n])

        n = 0
        while n < blocks:
            count = TILE // BLK if blocks - n > TILE // BLK else 2
            for r in range(0, span, TILE):
                rows = slice(r, r + TILE)
                first = top.shape[0]
                part_of = top[rows, :] if r < first else bottom[r - first : r - first + TILE, :]
                total = dot(part_of, panel[:, n * BLK : (n + count) * BLK])
                for m in range(count):
                    part = total[:, m * BLK : (m + 1) * BLK]
                    done[n + m, rows, :] = (base[rows, at(order[n + m])] - part).astype(BF16)
            for m in range(count):
                store(n + m).start()
            n += count
        for n in range(blocks):
            store(n).wait()

    return pl.pallas_call(
        kernel,
        out_shape=(out(1, span, span), out(*panel.shape)),
        in_specs=[SMEM] + [VMEM] * 5,
        out_specs=(HBM, VMEM),
        input_output_aliases={3: 1},
        scratch_shapes=[
            pltpu.SMEM((blocks,), jnp.int32),
            pltpu.VMEM((blocks, span, BLK), BF16),
            pltpu.SemaphoreType.DMA((blocks,)),
        ],
        compiler_params=params(14),
        cost_estimate=SMALL,
        name="update",
    )(child_map, *mults, panel, far, base)[0]


def body(front_matrix, kept_child, passed_child, child_map, pivots, pivot_inverse):
    hold = lax.optimization_barrier
    kid = kept_child.shape[1]
    arrived = flip(passed_child, "front", 1)
    u = early(child_map, pivots, front_matrix, kept_child)
    un, up = shift(u, "row", -1), shift(u, "row", 1)
    rows32, cols32 = prepare(child_map, pivots, front_matrix, kept_child)
    base = make_base(child_map, front_matrix, kept_child)
    arrived, _, rows32, cols32, base = hold((arrived, u, rows32, cols32, base))
    a, top, bottom, cross = extract(child_map, pivots, rows32, cols32, arrived)
    tfar, tnear = flip(top, "col", 2), flip(top, "col", 1)
    an, ap = shift(a, "row", -1), shift(a, "row", 1)
    cross2 = shift(cross, "row", 2)
    base = add_child(child_map, base, arrived)
    bfar, bnear = flip(bottom, "col", 2), flip(bottom, "col", 1)
    un, up, an, ap, cross2, base, tfar, tnear = hold((un, up, an, ap, cross2, base, tfar, tnear))
    panel, onward = stage((u, un, up), (a, an, ap))
    far = hand_on(onward)
    crosses = jnp.stack([cross, an[:BLK, kid:], cross2, ap[:BLK, kid:]])
    xfar, xnear = flip(crosses, "col", 2), flip(crosses, "col", 1)
    tcorners = [flip(tfar[n : n + PAIR], "col", 1) for n in range(0, top.shape[0], PAIR)]
    xfar, xnear, panel, tcorners, bfar, bnear = hold((xfar, xnear, panel, tcorners, bfar, bnear))
    xcorners = [flip(xfar[n : n + 2], "col", 1) for n in (0, 2)]
    first, second = begin((top, tnear, tfar), tcorners, pivot_inverse)
    first, second, xcorners = hold((first, second, xcorners))
    upper, x, k = multiply_top((crosses, xnear, xfar, *xcorners), first, second, pivot_inverse)
    bcorners = [flip(bfar[n : n + BLK], "col", 1) for n in range(0, bottom.shape[0], BLK)]
    upper, bcorners = hold((upper, bcorners))
    lower = multiply_bottom((bottom, bnear, bfar), bcorners, x, k, pivot_inverse)
    lower, far = hold((lower, far))
    return update(child_map, (upper, lower), panel, far, base)


def solution(mesh):
    in_specs = (
        P("front", "row", "col"),
        P("front", "row", "col"),
        P("front", "row", "col"),
        P("front", None, None),
        P("front", None, None),
        P("front", None, None, None),
    )
    out_specs = P("front", "row", "col")
    return jax.shard_map(body, mesh=mesh, in_specs=in_specs, out_specs=out_specs, check_vma=False)
```

```python
import jax
import jax.numpy as jnp
from jax import lax
from jax.experimental import pallas as pl
from jax.experimental.pallas import tpu as pltpu
from jax.sharding import PartitionSpec as P

BLK = 128
PAIR = 2 * BLK
TILE = 512
P_SIZE = 512
F32 = jnp.float32
BF16 = jnp.bfloat16
VMEM = pl.BlockSpec(memory_space=pltpu.VMEM)
HBM = pl.BlockSpec(memory_space=pltpu.HBM)
SMEM = pl.BlockSpec(memory_space=pltpu.SMEM)
MIB = 1 << 20
SMALL = pl.CostEstimate(flops=1000, bytes_accessed=1000, transcendentals=0)


def shift(x, axis, step):
    n = lax.axis_size(axis)
    return lax.ppermute(x, axis, [(i, (i + step) % n) for i in range(n)])


def flip(x, axis, bit):
    n = lax.axis_size(axis)
    return lax.ppermute(x, axis, [(i, i ^ bit) for i in range(n)])


def at(block, size=BLK):
    return pl.ds(pl.multiple_of(block * size, size), size)


def places():
    return lax.axis_index("row"), lax.axis_index("col")


def dot(a, b):
    return jnp.dot(a, b, preferred_element_type=F32)


def dot_t(a, b):
    return lax.dot_general(a, b, (((1,), (1,)), ((), ())), preferred_element_type=F32)


def out(*shape, dtype=BF16):
    return jax.ShapeDtypeStruct(shape, dtype)


def params(mib):
    return pltpu.CompilerParams(vmem_limit_bytes=mib * MIB)


def add_rows(acc, child, which, s, map_s, piv_s, row, col, here, kids):
    for k in range(kids):

        @pl.when(map_s[0, which, row * kids + k] == piv_s[0, s, row])
        def _():
            for a in range(kids):
                t = map_s[0, which, col * kids + a] - col * here
                acc[s, :, at(t)] += child[0, k * BLK : (k + 1) * BLK, a * BLK : (a + 1) * BLK].astype(F32)


def add_cols(acc, child, which, s, map_s, piv_s, row, col, here, kids):
    for k in range(kids):

        @pl.when(map_s[0, which, col * kids + k] == piv_s[0, s, col])
        def _():
            for a in range(kids):
                t = map_s[0, which, row * kids + a] - row * here
                acc[s, at(t), :] += child[0, a * BLK : (a + 1) * BLK, k * BLK : (k + 1) * BLK].astype(F32)


def scalars(map_ref, piv_ref, map_s, piv_s, sem):
    first = pltpu.make_async_copy(map_ref, map_s, sem.at[0])
    second = pltpu.make_async_copy(piv_ref, piv_s, sem.at[1])
    first.start()
    second.start()
    first.wait()
    second.wait()


def each_block(map_s, col, here, kids, visit):
    place = jnp.int32(0)
    for t in range(here):
        hit = jnp.bool_(False)
        for a in range(kids):
            hit = hit | (map_s[0, 1, col * kids + a] - col * here == t)

        @pl.when(jnp.logical_not(hit))
        def _():
            visit(t, place)

        place = place + jnp.where(hit, 0, 1)


def early_kernel(map_ref, piv_ref, front, kept, rows_out, map_s, piv_s, rows_in, kid, sem):
    row, col = places()
    here = front.shape[1] // BLK
    kids = kept.shape[1] // BLK
    child = pltpu.make_async_copy(kept, kid, sem.at[2])
    child.start()
    scalars(map_ref, piv_ref, map_s, piv_s, sem)
    copies = []
    for s in range(2):
        pr = piv_s[0, s, row] - row * here
        copies.append(pltpu.make_async_copy(front.at[0, at(pr), :], rows_in.at[s], sem.at[s]))
    for c in copies:
        c.start()
    for c in copies:
        c.wait()
    child.wait()
    for s in range(2):
        for k in range(kids):

            @pl.when(map_s[0, 0, row * kids + k] == piv_s[0, s, row])
            def _():
                for a in range(kids):
                    t = at(map_s[0, 0, col * kids + a] - col * here)
                    piece = kid[0, k * BLK : (k + 1) * BLK, a * BLK : (a + 1) * BLK].astype(F32)
                    rows_in[s, :, t] = (rows_in[s, :, t].astype(F32) + piece).astype(BF16)

    def visit(t, place):
        for s in range(2):
            rows_out[s * BLK : (s + 1) * BLK, at(place)] = rows_in[s, :, t * BLK : (t + 1) * BLK]

    each_block(map_s, col, here, kids, visit)


def early(child_map, pivots, front, kept):
    span = front.shape[1]
    return pl.pallas_call(
        early_kernel,
        out_shape=out(PAIR, span - kept.shape[1]),
        in_specs=[HBM] * 4,
        out_specs=VMEM,
        scratch_shapes=[
            pltpu.SMEM(child_map.shape, jnp.int32),
            pltpu.SMEM(pivots.shape, jnp.int32),
            pltpu.VMEM((2, BLK, span), BF16),
            pltpu.VMEM(kept.shape, BF16),
            pltpu.SemaphoreType.DMA((3,)),
        ],
        compiler_params=params(57),
        cost_estimate=SMALL,
        name="early",
    )(child_map, pivots, front, kept)


def prepare_kernel(
    map_ref, piv_ref, front, kept, rows_out, cols32, map_s, piv_s, rows_in, cols_in, rows32, sem
):
    row, col = places()
    here = front.shape[1] // BLK
    kids = kept.shape[1] // BLK
    scalars(map_ref, piv_ref, map_s, piv_s, sem)
    copies = []
    for s in range(2):
        pr = piv_s[0, s, row] - row * here
        pc = piv_s[0, s, col] - col * here
        copies.append(pltpu.make_async_copy(front.at[0, at(pr), :], rows_in.at[s], sem.at[2 * s]))
        copies.append(pltpu.make_async_copy(front.at[0, :, at(pc)], cols_in.at[s], sem.at[2 * s + 1]))
    for c in copies:
        c.start()
    for c in copies:
        c.wait()
    rows32[...] = rows_in[...].astype(F32)
    cols32[...] = cols_in[...].astype(F32)
    for s in range(2):
        add_rows(rows32, kept, 0, s, map_s, piv_s, row, col, here, kids)
        add_cols(cols32, kept, 0, s, map_s, piv_s, row, col, here, kids)
        for a in range(kids):
            t = map_s[0, 1, col * kids + a] - col * here
            rows_out[s, :, a * BLK : (a + 1) * BLK] = rows32[s, :, at(t)]


def prepare(child_map, pivots, front, kept):
    span = front.shape[1]
    return pl.pallas_call(
        prepare_kernel,
        out_shape=(out(2, BLK, kept.shape[1], dtype=F32), out(2, span, BLK, dtype=F32)),
        in_specs=[HBM, HBM, HBM, VMEM],
        out_specs=(VMEM, VMEM),
        scratch_shapes=[
            pltpu.SMEM(child_map.shape, jnp.int32),
            pltpu.SMEM(pivots.shape, jnp.int32),
            pltpu.VMEM((2, BLK, span), BF16),
            pltpu.VMEM((2, span, BLK), BF16),
            pltpu.VMEM((2, BLK, span), F32),
            pltpu.SemaphoreType.DMA((4,)),
        ],
        compiler_params=params(12),
        cost_estimate=SMALL,
        name="prepare",
    )(child_map, pivots, front, kept)


def extract_kernel(map_s, piv_s, rows32, cols32, arrived, rows_out, top, bottom, cross, cols):
    row, col = places()
    here = cols.shape[0] // BLK
    kids = arrived.shape[1] // BLK
    for s in range(2):
        own = slice(s * BLK, (s + 1) * BLK)
        rows_out[own, : kids * BLK] = rows32[s].astype(BF16)
        cols[:, own] = cols32[s].astype(BF16)
        for k in range(kids):

            @pl.when(map_s[0, 1, row * kids + k] == piv_s[0, s, row])
            def _():
                piece = arrived[0, k * BLK : (k + 1) * BLK, :].astype(F32)
                rows_out[own, : kids * BLK] = (rows32[s] + piece).astype(BF16)

            @pl.when(map_s[0, 1, col * kids + k] == piv_s[0, s, col])
            def _():
                for a in range(kids):
                    t = map_s[0, 1, row * kids + a] - row * here
                    piece = arrived[0, a * BLK : (a + 1) * BLK, k * BLK : (k + 1) * BLK].astype(F32)
                    cols[at(t), own] = (cols32[s, at(t), :] + piece).astype(BF16)

    top[...] = cols[: top.shape[0], :]
    bottom[...] = cols[top.shape[0] :, :]
    block = cols[at(piv_s[0, 1, row] - row * here), :BLK]
    rows_out[:BLK, kids * BLK :] = block
    rows_out[BLK:, kids * BLK :] = jnp.zeros((BLK, BLK), BF16)
    cross[...] = block


def extract(child_map, pivots, rows32, cols32, arrived):
    span = cols32.shape[1]
    return pl.pallas_call(
        extract_kernel,
        out_shape=(
            out(PAIR, arrived.shape[1] + BLK),
            out(span - TILE, PAIR),
            out(TILE, PAIR),
            out(BLK, BLK),
        ),
        in_specs=[SMEM] * 2 + [VMEM] * 3,
        out_specs=(VMEM,) * 4,
        scratch_shapes=[pltpu.VMEM((span, PAIR), BF16)],
        compiler_params=params(8),
        cost_estimate=SMALL,
        name="extract",
    )(child_map, pivots, rows32, cols32, arrived)


def add_blocks(base, child, which, map_s, first, deep):
    row, col = places()
    here = base.shape[1] // BLK
    kids = child.shape[1] // BLK
    for k in range(kids):
        t = map_s[0, which, row * kids + k] - row * here

        @pl.when((t >= first) & (t < first + deep))
        def _():
            for a in range(kids):
                u = map_s[0, which, col * kids + a] - col * here
                piece = child[0, k * BLK : (k + 1) * BLK, a * BLK : (a + 1) * BLK]
                base[at(t), at(u)] += piece.astype(F32)


def make_base(child_map, front, kept):
    span = front.shape[1]
    steps = 4
    width = span // steps

    def kernel(map_s, front, kept, base):
        step = pl.program_id(0)
        base[at(step, width), :] = front[0].astype(F32)
        add_blocks(base, kept, 0, map_s, step * (width // BLK), width // BLK)

    return pl.pallas_call(
        kernel,
        grid=(steps,),
        out_shape=out(span, span, dtype=F32),
        in_specs=[SMEM, pl.BlockSpec((1, width, span), lambda i: (0, i, 0)), VMEM],
        out_specs=VMEM,
        compiler_params=params(14),
        cost_estimate=SMALL,
        name="base",
    )(child_map, front, kept)


def add_child(child_map, base, arrived):
    def kernel(map_s, _, arrived, base):
        add_blocks(base, arrived, 1, map_s, 0, base.shape[0] // BLK)

    return pl.pallas_call(
        kernel,
        out_shape=out(*base.shape, dtype=F32),
        in_specs=[SMEM, VMEM, VMEM],
        out_specs=VMEM,
        input_output_aliases={1: 0},
        compiler_params=params(4),
        cost_estimate=SMALL,
        name="add_child",
    )(child_map, base, arrived)


def stage(us, as_):
    split = us[0].shape[1]
    kid = as_[0].shape[1] - BLK

    def kernel(u0, u1, u2, a0, a1, a2, panel, onward):
        _, col = places()
        even = lax.rem(col, 2) == 0
        for n, (u, a) in enumerate(((u0, a0), (u1, a1), (u2, a2))):
            panel[n * PAIR : (n + 1) * PAIR, :split] = u[...]
            panel[n * PAIR : (n + 1) * PAIR, split:] = a[:, :kid]

        @pl.when(even)
        def _():
            onward[:, :split] = u2[...]
            onward[:, split:] = a2[:, :kid]

        @pl.when(jnp.logical_not(even))
        def _():
            onward[:, :split] = u1[...]
            onward[:, split:] = a1[:, :kid]

    return pl.pallas_call(
        kernel,
        out_shape=(out(2 * P_SIZE, split + kid), out(PAIR, split + kid)),
        in_specs=[VMEM] * 6,
        out_specs=(VMEM, VMEM),
        compiler_params=params(4),
        cost_estimate=SMALL,
        name="stage",
    )(*us, *as_)


def hand_on(x):
    rows, cols = lax.axis_size("row"), lax.axis_size("col")
    route = []
    for r in range(rows):
        for c in range(cols):
            to = (r + 1) % rows if c % 2 == 0 else (r - 1) % rows
            route.append((r * cols + c, to * cols + c))
    return lax.ppermute(x, ("row", "col"), route)


def begin(pieces, corners, inverse):
    span = pieces[0].shape[0]

    def kernel(c0, c1, c2, *rest):
        *corners, inverse, first, second = rest
        _, col = places()
        js = [lax.bitwise_xor(col, q) for q in range(4)]
        for n, corner in enumerate(corners):
            rows = slice(n * PAIR, (n + 1) * PAIR)
            total = dot(corner[:, :BLK], inverse[0, 0, at(js[3]), :])
            second[rows, at(js[3])] = corner[:, BLK:]
            for q, c in enumerate((c0, c1, c2)):
                total += dot(c[rows, :BLK], inverse[0, 0, at(js[q]), :])
                second[rows, at(js[q])] = c[rows, BLK:]
            first[rows, :] = total

    return pl.pallas_call(
        kernel,
        out_shape=(out(span, P_SIZE, dtype=F32), out(span, P_SIZE)),
        in_specs=[VMEM] * (4 + len(corners)),
        out_specs=(VMEM, VMEM),
        compiler_params=params(6),
        cost_estimate=SMALL,
        name="begin",
    )(*pieces, *corners, inverse)


def ring_places(row):
    found = []
    for j in range(4):
        d = lax.rem(j - row + 4, 4)
        found.append(jnp.where(d < 2, d, 5 - d))
    return found


def eliminate(mult, rows, m1, i2, x, k, inverse, place):
    p2 = (i2.astype(F32) - dot_t(m1.astype(BF16), x[...])).astype(BF16)
    m2 = dot(p2, inverse[0, 1]).astype(BF16)
    n1 = (m1 - dot_t(m2, k[...])).astype(BF16)
    for j in range(4):
        b = slice(j * BLK, (j + 1) * BLK)
        mult[rows, at(2 * place[j])] = n1[:, b]
        mult[rows, at(2 * place[j] + 1)] = m2[:, b]


def multiply_top(crosses, first, second, inverse):
    span = first.shape[0]

    def kernel(x0, x1, x2, x3, x4, first, second, inverse, mult, x, k):
        row, col = places()
        for q, xq in enumerate((x0, x1, x2, (x3, x4))):
            j = lax.bitwise_xor(col, q)
            for d in range(4):
                x[at(lax.rem(row + d, 4)), at(j)] = xq[d // 2][d % 2] if q == 3 else xq[d]
        k[...] = dot_t(inverse[0, 0], x[...]).astype(BF16)
        place = ring_places(row)
        for r in range(0, span, TILE):
            rows = slice(r, r + TILE)
            eliminate(mult, rows, first[rows, :], second[rows, :], x, k, inverse, place)

    return pl.pallas_call(
        kernel,
        out_shape=(out(span, 2 * P_SIZE), out(P_SIZE, P_SIZE), out(P_SIZE, P_SIZE)),
        in_specs=[VMEM] * 8,
        out_specs=(VMEM,) * 3,
        compiler_params=params(8),
        cost_estimate=SMALL,
        name="multiply_top",
    )(*crosses, first, second, inverse)


def multiply_bottom(pieces, corners, x, k, inverse):
    span = pieces[0].shape[0]

    def kernel(c0, c1, c2, k0, k1, x, k, inverse, mult, p1, i2):
        row, col = places()
        for q, c in enumerate((c0, c1, c2)):
            j = lax.bitwise_xor(col, q)
            p1[:, at(j)] = c[:, :BLK]
            i2[:, at(j)] = c[:, BLK:]
        j = lax.bitwise_xor(col, 3)
        for n, corner in enumerate((k0, k1)):
            rows = slice(n * PAIR, (n + 1) * PAIR)
            p1[rows, at(j)] = corner[:, :BLK]
            i2[rows, at(j)] = corner[:, BLK:]
        m1 = dot(p1[...], inverse[0, 0])
        eliminate(mult, slice(0, span), m1, i2[...], x, k, inverse, ring_places(row))

    return pl.pallas_call(
        kernel,
        out_shape=out(span, 2 * P_SIZE),
        in_specs=[VMEM] * 8,
        out_specs=VMEM,
        scratch_shapes=[pltpu.VMEM((span, P_SIZE), BF16)] * 2,
        compiler_params=params(8),
        cost_estimate=SMALL,
        name="multiply_bottom",
    )(*pieces, *corners, x, k, inverse)


def update(child_map, mults, panel, far, base):
    span = base.shape[0]
    kids = child_map.shape[2] // 4
    blocks = span // BLK

    def kernel(map_s, top, bottom, _, far, base, updated, panel, order, done, sem):
        _, col = places()
        panel[3 * PAIR :, :] = far[...]

        def visit(t, place):
            order[place] = t

        each_block(map_s, col, blocks, kids, visit)
        for a in range(kids):
            order[blocks - kids + a] = map_s[0, 1, col * kids + a] - col * blocks

        def store(n):
            return pltpu.make_async_copy(done.at[n], updated.at[0, :, at(order[n])], sem.at[n])

        n = 0
        while n < blocks:
            count = TILE // BLK if blocks - n > TILE // BLK else 2
            for r in range(0, span, TILE):
                rows = slice(r, r + TILE)
                first = top.shape[0]
                part_of = top[rows, :] if r < first else bottom[r - first : r - first + TILE, :]
                total = dot(part_of, panel[:, n * BLK : (n + count) * BLK])
                for m in range(count):
                    part = total[:, m * BLK : (m + 1) * BLK]
                    done[n + m, rows, :] = (base[rows, at(order[n + m])] - part).astype(BF16)
            for m in range(count):
                store(n + m).start()
            n += count
        for n in range(blocks):
            store(n).wait()

    return pl.pallas_call(
        kernel,
        out_shape=(out(1, span, span), out(*panel.shape)),
        in_specs=[SMEM] + [VMEM] * 5,
        out_specs=(HBM, VMEM),
        input_output_aliases={3: 1},
        scratch_shapes=[
            pltpu.SMEM((blocks,), jnp.int32),
            pltpu.VMEM((blocks, span, BLK), BF16),
            pltpu.SemaphoreType.DMA((blocks,)),
        ],
        compiler_params=params(14),
        cost_estimate=SMALL,
        name="update",
    )(child_map, *mults, panel, far, base)[0]


def body(front_matrix, kept_child, passed_child, child_map, pivots, pivot_inverse):
    hold = lax.optimization_barrier
    kid = kept_child.shape[1]
    arrived = flip(passed_child, "front", 1)
    u = early(child_map, pivots, front_matrix, kept_child)
    un, up = shift(u, "row", -1), shift(u, "row", 1)
    rows32, cols32 = prepare(child_map, pivots, front_matrix, kept_child)
    base = make_base(child_map, front_matrix, kept_child)
    arrived, _, rows32, cols32, base = hold((arrived, u, rows32, cols32, base))
    a, top, bottom, cross = extract(child_map, pivots, rows32, cols32, arrived)
    tfar, tnear = flip(top, "col", 2), flip(top, "col", 1)
    an, ap = shift(a, "row", -1), shift(a, "row", 1)
    cross2 = shift(cross, "row", 2)
    base = add_child(child_map, base, arrived)
    un, up, an, ap, cross2, base, tfar, tnear, bottom = hold(
        (un, up, an, ap, cross2, base, tfar, tnear, bottom)
    )
    panel, onward = stage((u, un, up), (a, an, ap))
    far = hand_on(onward)
    crosses = jnp.stack([cross, an[:BLK, kid:], cross2, ap[:BLK, kid:]])
    xfar, xnear = flip(crosses, "col", 2), flip(crosses, "col", 1)
    bfar, bnear = flip(bottom, "col", 2), flip(bottom, "col", 1)
    tcorners = [flip(tfar[n : n + PAIR], "col", 1) for n in range(0, top.shape[0], PAIR)]
    xfar, xnear, panel, tcorners = hold((xfar, xnear, panel, tcorners))
    xcorners = [flip(xfar[n : n + 2], "col", 1) for n in (0, 2)]
    first, second = begin((top, tnear, tfar), tcorners, pivot_inverse)
    first, second, xcorners = hold((first, second, xcorners))
    upper, x, k = multiply_top((crosses, xnear, xfar, *xcorners), first, second, pivot_inverse)
    upper, bfar, bnear = hold((upper, bfar, bnear))
    bcorners = [flip(bfar[n : n + PAIR], "col", 1) for n in range(0, bottom.shape[0], PAIR)]
    lower = multiply_bottom((bottom, bnear, bfar), bcorners, x, k, pivot_inverse)
    lower, far = hold((lower, far))
    return update(child_map, (upper, lower), panel, far, base)


def solution(mesh):
    in_specs = (
        P("front", "row", "col"),
        P("front", "row", "col"),
        P("front", "row", "col"),
        P("front", None, None),
        P("front", None, None),
        P("front", None, None, None),
    )
    out_specs = P("front", "row", "col")
    return jax.shard_map(body, mesh=mesh, in_specs=in_specs, out_specs=out_specs, check_vma=False)
```
